1024 devices in a mesh: expert: 8 (over y_hi, core), tp: 128 (over y_lo, z, x).
Axes of the slice: x: 4, y: 8 (y_hi: 4, y_lo: 2; y = y_hi * 2 + y_lo), z: 16, core: 2. Of those that a mesh axis runs over, the one named last changes fastest.
Arguments:
- tokens: bfloat16 [512, 6144], P('expert', 'tp'), may hold values from -6 to 6
- routes: int32 [512, 2], P('expert'), may hold values from 0 to 7, all different within a row; in each aligned block of 64 rows (0 to 63, 64 to 127, ...) at most 32 rows name the same one
- w_gate: bfloat16 [8, 128, 1536, 4, 128], P('expert', 'tp'), may hold values from -0.078125 to 0.078125
- w_up: bfloat16 [8, 128, 1536, 4, 128], P('expert', 'tp'), may hold values from -0.078125 to 0.078125
- hidden_grad: bfloat16 [8, 256, 16384], P('expert', None, 'tp'), may hold values from -6 to 6
Outputs:
- token_grad: bfloat16 [512, 6144], P('expert', 'tp')
The draws below stay inside these ranges and needn't reach their ends.
Inputs may be any that keep to these rules, and one draw needn't show every extreme that they name: `routes`: the two experts of a token differ; among the 64 tokens of one expert-axis index no expert is named more than 32 times, and some expert exactly that often.
All inputs are finite; a program needn't handle non-finite values.
Results may differ from the reference program's by a relative error of at most 0.0059.
Values may be sent and summed in bfloat16 or wider, within the bound.
No kernel may reach another device: no remote copies, remote signals or barrier semaphores. Data moves between devices by JAX's collectives and lax.ppermute only.
A program may use at most 32 MiB of HBM per device.

```python
import math
import jax
import jax.numpy as jnp
import numpy as np
from jax import lax

D = 6144
FF = 16384
DG = 4
TOK_E = 64
EXPERTS = 8
FB = 32
HID_DEV = 128
WBLK = 1536
CAP_SRC = 32
TOKENS = 512
SLOTS = 256
N_EXPERT = 8


def steps_of(stream_key, extent, pieces, smallest, high):
    level, own = 1.0, jax.random.fold_in(stream_key, 6)
    for axis_at, parts in pieces:
        steps = jnp.exp(jax.random.uniform(jax.random.fold_in(own, axis_at), (parts,), jnp.float32, smallest / len(pieces), high / len(pieces)))
        level = level * jnp.repeat(steps, extent[axis_at] // parts).reshape([-1 if axis == axis_at else 1 for axis in range(len(extent))])
    return level


def deal_out(stream_key, own, number, rows, amount, top, reach, skew):
    ranking = jax.random.permutation(stream_key, amount)
    heavy_load, usual = shares(amount, rows * top, reach, skew, True), shares(amount, rows * top, reach, skew, False)
    places = jnp.arange(amount)

    def named(tallies, rotation):
        used = int((tallies > 0).sum())
        fixed = max(1, used // 4)
        passed = fixed + (places - fixed + rotation * (used - fixed)) % max(1, amount - fixed)
        return jnp.zeros((amount,), jnp.int32).at[ranking[jnp.where(places < fixed, places, passed)]].set(jnp.asarray(tallies, jnp.int32))

    tallies = jnp.where(number % 4 == 0, named(heavy_load, number // 4), named(usual, number - number // 4 - 1))
    mixed = jax.random.permutation(jax.random.fold_in(own, 3), amount)
    giver, sink = mixed[0:amount // 2 * 2:2], mixed[1:amount // 2 * 2:2]
    margin = jnp.minimum(tallies[giver] - 1, reach - tallies[sink]) // 2
    margin = jnp.where((giver == ranking[0]) | (sink == ranking[0]) | (tallies[sink] == 0), 0, jnp.maximum(margin, 0))
    passed = jax.random.randint(jax.random.fold_in(own, 4), (amount // 2,), 0, 1 << 20) % (margin + 1)
    tallies = tallies.at[giver].add(-passed).at[sink].add(passed)
    labels = jnp.searchsorted(jnp.cumsum(tallies), jnp.arange(rows * top), side="right").astype(jnp.int32)
    table = labels.reshape(top, rows).T
    table = table[jax.random.permutation(jax.random.fold_in(own, 1), rows)]
    rotation = jax.random.randint(jax.random.fold_in(own, 2), (rows, 1), 0, top)
    return jnp.take_along_axis(table, (jnp.arange(top)[None, :] + rotation) % top, axis=1)


def shares(number_of, total, bound, skew, full):
    loads = [(1 << 20) // math.isqrt(grade ** skew) + 1 for grade in range(1, number_of + 1)]
    largest = bound if full else min(bound, max(-(-total // number_of), total * loads[0] // sum(loads)))
    least = 1 if total - largest >= number_of - 1 else 0
    holding, surplus = [largest] + [least] * (number_of - 1), total - largest - least * (number_of - 1)
    while surplus > 0:
        candidates = [i for i in range(1, number_of) if holding[i] < largest] or [i for i in range(1, number_of) if holding[i] < bound]
        whole, budget = sum([loads[i] for i in candidates]), surplus
        for i in candidates:
            more = min(bound - holding[i], max(1, budget * loads[i] // whole), surplus)
            holding[i] = holding[i] + more
            surplus = surplus - more
    return np.array(holding)


def normal_values(rng, dims, spread, reach, shards=(), kind=jnp.bfloat16):
    drawn = jax.random.normal(rng, dims, jnp.float32) * spread
    if len(shards) > 0:
        drawn = steps_of(rng, dims, shards, -0.22, 0.18) * drawn
    return jnp.clip(drawn, min=-reach, max=reach).astype(kind)


def setup_inputs(seed: int = 0) -> dict:
    keys = jax.random.split(jax.random.key(seed), 6)
    tokens = normal_values(keys[0], (TOKENS, D), 1.0, 6.0, ((0, 8), (1, 128)))
    routes_keys = jax.random.split(jax.random.fold_in(keys[1], 1), TOKENS // TOK_E)
    routes_turns = jax.random.permutation(jax.random.fold_in(keys[1], 3), TOKENS // TOK_E)
    routes = jax.vmap(lambda own, number: deal_out(jax.random.fold_in(keys[1], 2), own, number, TOK_E, EXPERTS, 2, CAP_SRC, 2))(routes_keys, routes_turns).reshape((TOKENS, 2))
    w_gate = normal_values(keys[2], (EXPERTS, DG * FB, WBLK, DG, HID_DEV), D ** -0.5, 0.078125, ((0, 8), (1, 128)))
    w_up = normal_values(keys[3], (EXPERTS, DG * FB, WBLK, DG, HID_DEV), D ** -0.5, 0.078125, ((0, 8), (1, 128)))
    hidden_grad = normal_values(keys[4], (EXPERTS, SLOTS, FF), 1.0, 6.0, ((0, 8), (2, 128)))
    return {"tokens": tokens, "routes": routes, "w_gate": w_gate, "w_up": w_up, "hidden_grad": hidden_grad}


def slot_table(routes):
    expert_iota = jnp.arange(EXPERTS, dtype=jnp.int32)
    flat_routes = routes.reshape(N_EXPERT, TOK_E * 2)
    one_hot = (flat_routes[:, :, None] == expert_iota[None, None, :]).astype(jnp.int32)
    before = (jnp.cumsum(one_hot, axis=1) - one_hot).astype(jnp.int32)
    position = jnp.sum(before * one_hot, axis=2).astype(jnp.int32)
    source = jnp.arange(N_EXPERT, dtype=jnp.int32)[:, None]
    return (source * CAP_SRC + position).astype(jnp.int32).reshape(TOKENS, 2)


def full_matrix(blocks):
    shaped = blocks.reshape(DG, FB, WBLK, DG, HID_DEV)
    return jnp.transpose(shaped, (0, 2, 3, 1, 4)).reshape(D, FF)


def expert_backward(expert_item):
    slot_rows, gate_blocks, up_blocks, grad_hidden = expert_item
    gate_weight = full_matrix(gate_blocks)
    up_weight = full_matrix(up_blocks)
    gate_pre = jnp.dot(slot_rows, gate_weight, preferred_element_type=jnp.float32)
    up_pre = jnp.dot(slot_rows, up_weight, preferred_element_type=jnp.float32)
    sigmoid_gate = jax.nn.sigmoid(gate_pre)
    upstream = grad_hidden.astype(jnp.float32)
    gate_grad = (upstream * up_pre * sigmoid_gate * (1.0 + gate_pre * (1.0 - sigmoid_gate))).astype(jnp.bfloat16)
    up_grad = (upstream * gate_pre * sigmoid_gate).astype(jnp.bfloat16)
    summed = jnp.dot(gate_grad, gate_weight.T, preferred_element_type=jnp.float32)
    summed = summed + jnp.dot(up_grad, up_weight.T, preferred_element_type=jnp.float32)
    return summed.astype(jnp.bfloat16)


def reference(tokens, routes, w_gate, w_up, hidden_grad):
    slot_index = slot_table(routes)
    copies = jnp.broadcast_to(tokens[:, None, :], (TOKENS, 2, D))
    buffer = jnp.zeros((EXPERTS, SLOTS, D), jnp.bfloat16).at[routes, slot_index].set(copies)
    slot_grad = lax.map(expert_backward, (buffer, w_gate, w_up, hidden_grad))
    picked = slot_grad[routes, slot_index].astype(jnp.float32)
    return jnp.sum(picked, axis=1).astype(jnp.bfloat16)
```

```python
import jax
import jax.numpy as jnp
from jax import lax
from jax.sharding import PartitionSpec as P

NX, NZL = 4, 8
X_GROUPS = [[b * NX + x for x in range(NX)] for b in range(32)]
ZL_GROUPS = [
    [hi * 32 + zl * NX + x for zl in range(NZL)] for hi in range(4) for x in range(NX)
]
Y_BIT, ZH_BIT = 64, 32


def swapped(shard, bit):
    return lax.ppermute(shard, "tp", [(i, i ^ bit) for i in range(lax.axis_size("tp"))])


def body(tokens, routes, w_gate, w_up, hidden_grad):
    f32, bf16 = jnp.float32, jnp.bfloat16
    position = lax.axis_index("tp")
    is_y0 = jnp.bitwise_and(position, Y_BIT) == 0
    is_zh0 = jnp.bitwise_and(position, ZH_BIT) == 0
    n_groups = lax.axis_size("expert")
    slot_total = hidden_grad.shape[1]
    capacity = slot_total // n_groups
    n_tok, feat = tokens.shape
    block_rows = w_gate.shape[2]
    hid = w_gate.shape[4]
    wide = NZL * feat

    turned = tokens.T
    packed = jnp.concatenate([turned[: feat // 2], turned[feat // 2 :]], axis=1)
    raw = lax.all_to_all(
        jnp.broadcast_to(packed[None], (NZL,) + packed.shape),
        "tp",
        split_axis=0,
        concat_axis=0,
        axis_index_groups=ZL_GROUPS,
        tiled=True,
    )
    raw = jnp.concatenate([raw[:, :, :n_tok], raw[:, :, n_tok:]], axis=1).reshape(wide, n_tok)

    flat_routes = routes.reshape(n_tok * 2)
    one_hot = (flat_routes[:, None] == jnp.arange(n_groups, dtype=jnp.int32)[None, :]).astype(jnp.int32)
    before = jnp.cumsum(one_hot, axis=0) - one_hot
    slot_index = (flat_routes * capacity + jnp.sum(before * one_hot, axis=1)).reshape(n_tok, 2)
    slots = jnp.arange(slot_total, dtype=jnp.int32)[:, None]
    placing = ((slots == slot_index[None, :, 0]) | (slots == slot_index[None, :, 1])).astype(bf16)

    outgoing = lax.dot_general(
        placing, raw, (((1,), (1,)), ((), ())), preferred_element_type=f32
    ).astype(bf16)
    arrived = lax.all_to_all(outgoing, "expert", split_axis=0, concat_axis=0, tiled=True)
    rows = lax.all_gather(arrived, "tp", axis_index_groups=X_GROUPS, axis=0, tiled=False)
    rows = rows.transpose(1, 0, 2).reshape(slot_total, block_rows)

    both = jnp.stack([w_gate[0, 0], w_up[0, 0]])
    both = both.reshape(2, NZL, NX, feat, 2, 2, hid)
    both = both.transpose(2, 1, 3, 4, 0, 5, 6).reshape(block_rows, 8 * hid)

    pre = jnp.dot(rows, both, preferred_element_type=f32)
    half = 4 * hid
    keep = jnp.where(is_y0, pre[:, :half], pre[:, half:])
    send = jnp.where(is_y0, pre[:, half:], pre[:, :half]).astype(bf16)
    hidden, send = lax.optimization_barrier((hidden_grad[0], send))
    got = swapped(send, Y_BIT)
    hidden_other = swapped(hidden, ZH_BIT)
    keep = keep + got.astype(f32)
    keep = keep + swapped(keep.astype(bf16), ZH_BIT).astype(f32)

    upstream = jnp.concatenate(
        [jnp.where(is_zh0, hidden, hidden_other), jnp.where(is_zh0, hidden_other, hidden)], axis=1
    ).astype(f32)
    gate_pre, up_pre = keep[:, : 2 * hid], keep[:, 2 * hid :]
    sigmoid_gate = jax.nn.sigmoid(gate_pre)
    gate_grad = upstream * up_pre * sigmoid_gate * (1.0 + gate_pre * (1.0 - sigmoid_gate))
    up_grad = upstream * gate_pre * sigmoid_gate
    grads = jnp.concatenate([gate_grad.astype(bf16), up_grad.astype(bf16)], axis=1)
    other = swapped(grads, Y_BIT)
    grads = jnp.concatenate([jnp.where(is_y0, grads, other), jnp.where(is_y0, other, grads)], axis=1)

    partial_sum = lax.dot_general(
        grads, both, (((1,), (1,)), ((), ())), preferred_element_type=f32
    ).astype(bf16)
    pieces = partial_sum.reshape(slot_total, NX, wide).transpose(1, 0, 2)
    pieces = lax.all_to_all(
        pieces, "tp", split_axis=0, concat_axis=0, axis_index_groups=X_GROUPS, tiled=True
    )
    summed = jnp.sum(pieces.astype(f32), axis=0).astype(bf16)
    returned = lax.all_to_all(summed, "expert", split_axis=0, concat_axis=0, tiled=True)

    token_part = lax.dot_general(
        returned, placing, (((0,), (0,)), ((), ())), preferred_element_type=f32
    ).reshape(NZL, feat, n_tok)
    token_part = jnp.concatenate([token_part[:, : feat // 2], token_part[:, feat // 2 :]], axis=2)
    token_part = lax.all_to_all(
        token_part, "tp", split_axis=0, concat_axis=0, axis_index_groups=ZL_GROUPS, tiled=True
    )
    total = jnp.sum(token_part, axis=0)
    total = jnp.concatenate([total[:, :n_tok], total[:, n_tok:]], axis=0)
    return total.T.astype(bf16)


def solution(mesh):
    placed = (
        P("expert", "tp"),
        P("expert", None),
        P("expert", "tp", None, None, None),
        P("expert", "tp", None, None, None),
        P("expert", None, "tp"),
    )
    return jax.shard_map(
        body, mesh=mesh, in_specs=placed, out_specs=P("expert", "tp"), check_vma=False
    )
```

```python
import jax
import jax.numpy as jnp
from jax import lax
from jax.experimental import pallas as pl
from jax.experimental.pallas import tpu as pltpu
from jax.sharding import PartitionSpec as P

NX, NZL = 4, 8
X_GROUPS = [[b * NX + x for x in range(NX)] for b in range(32)]
ZL_GROUPS = [
    [hi * 32 + zl * NX + x for zl in range(NZL)] for hi in range(4) for x in range(NX)
]
Y_BIT, ZH_BIT = 64, 32
F32, BF16 = jnp.float32, jnp.bfloat16
NT = (((1,), (1,)), ((), ()))
TN = (((0,), (0,)), ((), ()))
VMEM = pl.BlockSpec(memory_space=pltpu.VMEM)
SMEM = pl.BlockSpec(memory_space=pltpu.SMEM)


def call(kernel, out_shape, n_scalar, n_array, flops=0, moved=0, mib=6):
    several = isinstance(out_shape, (tuple, list))
    return pl.pallas_call(
        kernel,
        out_shape=out_shape,
        in_specs=[SMEM] * n_scalar + [VMEM] * n_array,
        out_specs=[VMEM] * len(out_shape) if several else VMEM,
        compiler_params=pltpu.CompilerParams(vmem_limit_bytes=mib * 1024 * 1024),
        cost_estimate=pl.CostEstimate(flops=flops, bytes_accessed=moved, transcendentals=0),
    )


def swapped(shard, bit):
    return lax.ppermute(shard, "tp", [(i, i ^ bit) for i in range(lax.axis_size("tp"))])


def over(axis, shard, groups=None):
    return lax.all_to_all(
        shard, axis, split_axis=0, concat_axis=0, axis_index_groups=groups, tiled=True
    )


def dot(a, b, dims=(((1,), (0,)), ((), ()))):
    return lax.dot_general(a, b, dims, preferred_element_type=F32)


def pack_kernel(tok_ref, out_ref):
    turned = tok_ref[...]
    third = turned.shape[0] // 3
    packed = jnp.concatenate([turned[j * third : (j + 1) * third] for j in range(3)], axis=1)
    for z in range(out_ref.shape[0]):
        out_ref[z] = packed


def one_hot(slot_ref, slot_total):
    n_tok = slot_ref.shape[1]
    slots = lax.broadcasted_iota(jnp.int32, (slot_total, n_tok), 0)
    hit = (slots == slot_ref[0:1, :]) | (slots == slot_ref[1:2, :])
    return jnp.where(hit, 1.0, 0.0).astype(BF16)


def dispatch_kernel(slot_ref, raw_ref, out_ref):
    n_tok = slot_ref.shape[1]
    pieces = [
        raw_ref[z, :, j * n_tok : (j + 1) * n_tok] for z in range(raw_ref.shape[0]) for j in range(3)
    ]
    raw = jnp.concatenate(pieces, axis=0)
    out_ref[...] = dot(one_hot(slot_ref, out_ref.shape[0]), raw, NT).astype(BF16)


def halves(y_ref, width):
    own = pl.multiple_of(y_ref[0] * width, width)
    other = pl.multiple_of((1 - y_ref[0]) * width, width)
    return pl.ds(own, width), pl.ds(other, width)


def forward_kernel(y_ref, rows_ref, gate_ref, up_ref, keep_ref, send_ref):
    width = gate_ref.shape[1] // 2
    own, other = halves(y_ref, width)
    rows = jnp.concatenate([rows_ref[x] for x in range(rows_ref.shape[0])], axis=1)
    for m, w_ref in enumerate((gate_ref, up_ref)):
        at = slice(m * width, (m + 1) * width)
        send_ref[:, at] = dot(rows, w_ref[:, other]).astype(BF16)
        keep_ref[:, at] = dot(rows, w_ref[:, own])


def grad_kernel(zh_ref, keep_ref, near_ref, got_ref, hid_ref, far_ref, out_ref):
    hid = hid_ref.shape[1]
    total = keep_ref[...] + near_ref[...].astype(F32) + got_ref[...].astype(F32)
    for j in range(2):
        mine = zh_ref[0] == j
        upstream = jnp.where(mine, hid_ref[...].astype(F32), far_ref[...].astype(F32))
        gate_pre = total[:, j * hid : (j + 1) * hid]
        up_pre = total[:, (2 + j) * hid : (3 + j) * hid]
        sig = jax.nn.sigmoid(gate_pre)
        gate_grad = upstream * up_pre * sig * (1.0 + gate_pre * (1.0 - sig))
        out_ref[:, j * hid : (j + 1) * hid] = gate_grad.astype(BF16)
        out_ref[:, (2 + j) * hid : (3 + j) * hid] = (upstream * gate_pre * sig).astype(BF16)


def backward_kernel(y_ref, own_ref, other_ref, gate_ref, up_ref, out_ref):
    width = gate_ref.shape[1] // 2
    own, other = halves(y_ref, width)
    wide = out_ref.shape[2]
    for x in range(out_ref.shape[0]):
        at = slice(x * wide, (x + 1) * wide)
        total = dot(own_ref[:, :width], gate_ref[at, own], NT)
        total = total + dot(own_ref[:, width:], up_ref[at, own], NT)
        total = total + dot(other_ref[:, :width], gate_ref[at, other], NT)
        total = total + dot(other_ref[:, width:], up_ref[at, other], NT)
        out_ref[x] = total.astype(BF16)


def sum_kernel(pieces_ref, out_ref):
    total = pieces_ref[0].astype(F32)
    for x in range(1, pieces_ref.shape[0]):
        total = total + pieces_ref[x].astype(F32)
    out_ref[...] = total.astype(BF16)


def combine_kernel(slot_ref, back_ref, out_ref):
    placing = one_hot(slot_ref, back_ref.shape[0])
    part = dot(back_ref[...], placing, TN)
    half = out_ref.shape[1]
    for z in range(out_ref.shape[0]):
        low = part[2 * z * half : (2 * z + 1) * half]
        out_ref[z] = jnp.concatenate([low, part[(2 * z + 1) * half : (2 * z + 2) * half]], axis=1)


def finish_kernel(part_ref, out_ref):
    total = part_ref[0]
    for z in range(1, part_ref.shape[0]):
        total = total + part_ref[z]
    n_tok = out_ref.shape[1]
    out_ref[...] = jnp.concatenate([total[:, :n_tok], total[:, n_tok:]], axis=0).astype(BF16)


def body(tokens, routes, w_gate, w_up, hidden_grad):
    position = lax.axis_index("tp")
    y_at = jnp.bitwise_and(jnp.right_shift(position, 6), 1).reshape(1)
    zh_at = jnp.bitwise_and(jnp.right_shift(position, 5), 1).reshape(1)
    n_groups = lax.axis_size("expert")
    slot_total = hidden_grad.shape[1]
    capacity = slot_total // n_groups
    n_tok, feat = tokens.shape
    block_rows = w_gate.shape[2]
    hid = w_gate.shape[4]
    wide = NZL * feat
    shape = jax.ShapeDtypeStruct

    packed = call(pack_kernel, shape((NZL, feat // 3, 3 * n_tok), BF16), 0, 1)(tokens.T)
    raw = over("tp", packed, ZL_GROUPS)
    hidden = hidden_grad[0]
    raw, hidden_send = lax.optimization_barrier((raw, hidden))

    flat_routes = routes.reshape(n_tok * 2)
    named = (flat_routes[:, None] == jnp.arange(n_groups, dtype=jnp.int32)[None, :]).astype(jnp.int32)
    before = jnp.cumsum(named, axis=0) - named
    slot_index = flat_routes * capacity + jnp.sum(before * named, axis=1)
    slot_index = slot_index.reshape(n_tok, 2).T

    outgoing = call(dispatch_kernel, shape((slot_total, wide), BF16), 0, 2)(slot_index, raw)
    arrived = over("expert", outgoing)
    rows = over("tp", jnp.broadcast_to(arrived[None], (NX, slot_total, wide)), X_GROUPS)
    hidden_far = swapped(hidden_send, ZH_BIT)
    rows, hidden_far = lax.optimization_barrier((rows, hidden_far))

    def arranged(w):
        w = w[0, 0].reshape(NZL, NX, feat, 4, hid).transpose(1, 0, 2, 3, 4)
        return w.reshape(block_rows, 4 * hid)

    gate, up = arranged(w_gate), arranged(w_up)

    half = 4 * hid
    n_flops = 2 * slot_total * block_rows * 2 * half
    n_bytes = 4 * block_rows * half
    keep, send = call(
        forward_kernel,
        [shape((slot_total, half), F32), shape((slot_total, half), BF16)],
        1,
        3,
        n_flops,
        n_bytes,
        16,
    )(y_at, rows, gate, up)
    near = swapped(send, Y_BIT)
    got = swapped((keep + near.astype(F32)).astype(BF16), ZH_BIT)

    grads = call(grad_kernel, shape((slot_total, half), BF16), 1, 5)(
        zh_at, keep, near, got, hidden, hidden_far
    )
    other = swapped(grads, Y_BIT)
    pieces = call(
        backward_kernel, shape((NX, slot_total, wide), BF16), 1, 4, n_flops, n_bytes, 16
    )(y_at, grads, other, gate, up)
    pieces = over("tp", pieces, X_GROUPS)
    summed = call(sum_kernel, shape((slot_total, wide), BF16), 0, 1)(pieces)
    returned = over("expert", summed)

    part = call(combine_kernel, shape((NZL, feat // 2, 2 * n_tok), F32), 0, 2)(slot_index, returned)
    part = over("tp", part, ZL_GROUPS)
    total = call(finish_kernel, shape((feat, n_tok), BF16), 0, 1)(part)
    return total.T


def solution(mesh):
    placed = (
        P("expert", "tp"),
        P("expert", None),
        P("expert", "tp", None, None, None),
        P("expert", "tp", None, None, None),
        P("expert", None, "tp"),
    )
    return jax.shard_map(
        body, mesh=mesh, in_specs=placed, out_specs=P("expert", "tp"), check_vma=False
    )
```

```python
import functools

import jax
import jax.numpy as jnp
from jax import lax
from jax.experimental import pallas as pl
from jax.experimental.pallas import tpu as pltpu
from jax.sharding import PartitionSpec as P

NX, NZL = 4, 8
X_GROUPS = [[b * NX + x for x in range(NX)] for b in range(32)]
ZH_GROUPS = [
    [y * 64 + zh * 32 + f for zh in range(2)] for y in range(2) for f in range(32)
]
ZL_GROUPS = [
    [hi * 32 + zl * NX + x for zl in range(NZL)] for hi in range(4) for x in range(NX)
]
Y_BIT = 64
F32, BF16 = jnp.float32, jnp.bfloat16
NT = (((1,), (1,)), ((), ()))
TN = (((0,), (0,)), ((), ()))
VMEM = pl.BlockSpec(memory_space=pltpu.VMEM)
SMEM = pl.BlockSpec(memory_space=pltpu.SMEM)


def call(kernel, outs, scalars, arrays, flops=0, mib=6):
    several = isinstance(outs, (tuple, list))
    moved = sum(v.size * v.dtype.itemsize for v in [*arrays, *(outs if several else [outs])])
    return pl.pallas_call(
        kernel,
        out_shape=outs,
        in_specs=[SMEM] * len(scalars) + [VMEM] * len(arrays),
        out_specs=[VMEM] * len(outs) if several else VMEM,
        compiler_params=pltpu.CompilerParams(vmem_limit_bytes=mib * 1024 * 1024),
        cost_estimate=pl.CostEstimate(flops=flops, bytes_accessed=moved, transcendentals=0),
    )(*scalars, *arrays)


def swapped(shard, bit):
    return lax.ppermute(shard, "tp", [(i, i ^ bit) for i in range(lax.axis_size("tp"))])


def over(axis, shard, groups=None):
    return lax.all_to_all(
        shard, axis, split_axis=0, concat_axis=0, axis_index_groups=groups, tiled=True
    )


def dot(a, b, dims=(((1,), (0,)), ((), ()))):
    return lax.dot_general(a, b, dims, preferred_element_type=F32)


def pack_kernel(tok_ref, out_ref):
    turned = tok_ref[...]
    third = turned.shape[0] // 3
    packed = jnp.concatenate([turned[j * third : (j + 1) * third] for j in range(3)], axis=1)
    for z in range(out_ref.shape[0]):
        out_ref[z] = packed


def arrange_kernel(gate_ref, up_ref, gate_out_ref, up_out_ref):
    feat = gate_ref.shape[0] // (NX * NZL)
    for x in range(NX):
        for z in range(NZL):
            src, dst = (z * NX + x) * feat, (x * NZL + z) * feat
            gate_out_ref[dst : dst + feat] = gate_ref[src : src + feat]
            up_out_ref[dst : dst + feat] = up_ref[src : src + feat]


def one_hot(slot_ref, slot_total):
    n_tok = slot_ref.shape[1]
    slots = lax.broadcasted_iota(jnp.int32, (slot_total, n_tok), 0)
    hit = (slots == slot_ref[0:1, :]) | (slots == slot_ref[1:2, :])
    return jnp.where(hit, 1.0, 0.0).astype(BF16)


def dispatch_kernel(slot_ref, raw_ref, out_ref):
    n_tok = slot_ref.shape[1]
    pieces = [
        raw_ref[z, :, j * n_tok : (j + 1) * n_tok] for z in range(raw_ref.shape[0]) for j in range(3)
    ]
    raw = jnp.concatenate(pieces, axis=0)
    out_ref[...] = dot(one_hot(slot_ref, out_ref.shape[0]), raw, NT).astype(BF16)


def halves(y_ref, width):
    own = pl.multiple_of(y_ref[0] * width, width)
    other = pl.multiple_of((1 - y_ref[0]) * width, width)
    return pl.ds(own, width), pl.ds(other, width)


def forward_kernel(y_ref, rows_ref, gate_ref, up_ref, out_ref, *, mine):
    width = gate_ref.shape[1] // 2
    at = halves(y_ref, width)[0 if mine else 1]
    rows = jnp.concatenate([rows_ref[x] for x in range(rows_ref.shape[0])], axis=1)
    for m, w_ref in enumerate((gate_ref, up_ref)):
        out_ref[:, m * width : (m + 1) * width] = dot(rows, w_ref[:, at]).astype(out_ref.dtype)


def near_kernel(keep_ref, near_ref, hid_ref, total_ref, send_ref):
    total = keep_ref[...] + near_ref[...].astype(F32)
    width = total.shape[1]
    total_ref[...] = total
    send_ref[:, :width] = total.astype(BF16)
    send_ref[:, width:] = hid_ref[...]


def grad_kernel(zh_ref, total_ref, both_ref, out_ref):
    width = total_ref.shape[1]
    hid = width // 4
    total = total_ref[...] + both_ref[1 - zh_ref[0], :, :width].astype(F32)
    for j in range(2):
        upstream = both_ref[j, :, width:].astype(F32)
        gate_pre = total[:, j * hid : (j + 1) * hid]
        up_pre = total[:, (2 + j) * hid : (3 + j) * hid]
        sig = jax.nn.sigmoid(gate_pre)
        gate_grad = upstream * up_pre * sig * (1.0 + gate_pre * (1.0 - sig))
        out_ref[:, j * hid : (j + 1) * hid] = gate_grad.astype(BF16)
        out_ref[:, (2 + j) * hid : (3 + j) * hid] = (upstream * gate_pre * sig).astype(BF16)


def backward_kernel(y_ref, grad_ref, gate_ref, up_ref, *rest, mine):
    out_ref = rest[-1]
    width = gate_ref.shape[1] // 2
    at = halves(y_ref, width)[0 if mine else 1]
    wide = out_ref.shape[2]
    for x in range(out_ref.shape[0]):
        r = slice(x * wide, (x + 1) * wide)
        total = dot(grad_ref[:, :width], gate_ref[r, at], NT)
        total = total + dot(grad_ref[:, width:], up_ref[r, at], NT)
        if not mine:
            total = total + rest[0][x]
        out_ref[x] = total.astype(out_ref.dtype)


def sum_kernel(pieces_ref, out_ref):
    total = pieces_ref[0].astype(F32)
    for x in range(1, pieces_ref.shape[0]):
        total = total + pieces_ref[x].astype(F32)
    out_ref[...] = total.astype(BF16)


def combine_kernel(slot_ref, back_ref, out_ref):
    placing = one_hot(slot_ref, back_ref.shape[0])
    part = dot(back_ref[...], placing, TN)
    half = out_ref.shape[1]
    for z in range(out_ref.shape[0]):
        low = part[2 * z * half : (2 * z + 1) * half]
        out_ref[z] = jnp.concatenate([low, part[(2 * z + 1) * half : (2 * z + 2) * half]], axis=1)


def finish_kernel(part_ref, out_ref):
    total = part_ref[0]
    for z in range(1, part_ref.shape[0]):
        total = total + part_ref[z]
    n_tok = out_ref.shape[1]
    out_ref[...] = jnp.concatenate([total[:, :n_tok], total[:, n_tok:]], axis=0).astype(BF16)


def body(tokens, routes, w_gate, w_up, hidden_grad):
    position = lax.axis_index("tp")
    y_at = jnp.bitwise_and(jnp.right_shift(position, 6), 1).reshape(1)
    zh_at = jnp.bitwise_and(jnp.right_shift(position, 5), 1).reshape(1)
    n_groups = lax.axis_size("expert")
    slot_total = hidden_grad.shape[1]
    capacity = slot_total // n_groups
    n_tok, feat = tokens.shape
    block_rows = w_gate.shape[2]
    hid = w_gate.shape[4]
    wide = NZL * feat
    shape = jax.ShapeDtypeStruct

    half = 4 * hid
    flat = [w[0, 0].reshape(block_rows, half) for w in (w_gate, w_up)]
    gate, up = call(arrange_kernel, [shape((block_rows, half), BF16)] * 2, [], flat, mib=16)

    packed = call(pack_kernel, shape((NZL, feat // 3, 3 * n_tok), BF16), [], [tokens.T])
    raw = over("tp", packed, ZL_GROUPS)

    flat_routes = routes.reshape(n_tok * 2)
    named = (flat_routes[:, None] == jnp.arange(n_groups, dtype=jnp.int32)[None, :]).astype(jnp.int32)
    before = jnp.cumsum(named, axis=0) - named
    slot_index = flat_routes * capacity + jnp.sum(before * named, axis=1)
    slot_index = slot_index.reshape(n_tok, 2).T

    outgoing = call(dispatch_kernel, shape((slot_total, wide), BF16), [], [slot_index, raw])
    arrived = over("expert", outgoing)
    arrived, gate, up = lax.optimization_barrier((arrived, gate, up))
    rows = lax.all_gather(arrived, "tp", axis_index_groups=X_GROUPS, axis=0, tiled=False)

    n_flops = 2 * slot_total * block_rows * half
    given = [rows, gate, up]
    send = call(
        functools.partial(forward_kernel, mine=False),
        shape((slot_total, half), BF16),
        [y_at],
        given,
        n_flops,
        16,
    )
    keep = call(
        functools.partial(forward_kernel, mine=True),
        shape((slot_total, half), F32),
        [y_at],
        given,
        n_flops,
        16,
    )
    near = swapped(send, Y_BIT)
    total, send = call(
        near_kernel,
        [shape((slot_total, half), F32), shape((slot_total, half + hid), BF16)],
        [],
        [keep, near, hidden_grad[0]],
    )
    both = lax.all_gather(send, "tp", axis_index_groups=ZH_GROUPS, axis=0, tiled=False)

    grads = call(grad_kernel, shape((slot_total, half), BF16), [zh_at], [total, both])
    other = swapped(grads, Y_BIT)
    pieces = (NX, slot_total, wide)
    held = call(
        functools.partial(backward_kernel, mine=True),
        shape(pieces, F32),
        [y_at],
        [grads, gate, up],
        n_flops,
        16,
    )
    pieces = call(
        functools.partial(backward_kernel, mine=False),
        shape(pieces, BF16),
        [y_at],
        [other, gate, up, held],
        n_flops,
        16,
    )
    pieces = over("tp", pieces, X_GROUPS)
    summed = call(sum_kernel, shape((slot_total, wide), BF16), [], [pieces])
    returned = over("expert", summed)

    part = call(combine_kernel, shape((NZL, feat // 2, 2 * n_tok), F32), [], [slot_index, returned])
    part = over("tp", part, ZL_GROUPS)
    total = call(finish_kernel, shape((feat, n_tok), BF16), [], [part])
    return total.T


def solution(mesh):
    placed = (
        P("expert", "tp"),
        P("expert", None),
        P("expert", "tp", None, None, None),
        P("expert", "tp", None, None, None),
        P("expert", None, "tp"),
    )
    return jax.shard_map(
        body, mesh=mesh, in_specs=placed, out_specs=P("expert", "tp"), check_vma=False
    )
```

```python
import functools

import jax
import jax.numpy as jnp
from jax import lax
from jax.experimental import pallas as pl
from jax.experimental.pallas import tpu as pltpu
from jax.sharding import PartitionSpec as P

NX, NZL = 4, 8
X_GROUPS = [[b * NX + x for x in range(NX)] for b in range(32)]
ZL_GROUPS = [
    [hi * 32 + zl * NX + x for zl in range(NZL)] for hi in range(4) for x in range(NX)
]
Y_BIT, ZH_BIT = 64, 32
F32, BF16 = jnp.float32, jnp.bfloat16
NT = (((1,), (1,)), ((), ()))
TN = (((0,), (0,)), ((), ()))
VMEM = pl.BlockSpec(memory_space=pltpu.VMEM)
SMEM = pl.BlockSpec(memory_space=pltpu.SMEM)


def call(kernel, outs, scalars, arrays, flops=0, mib=6):
    several = isinstance(outs, (tuple, list))
    moved = sum(v.size * v.dtype.itemsize for v in [*arrays, *(outs if several else [outs])])
    return pl.pallas_call(
        kernel,
        out_shape=outs,
        in_specs=[SMEM] * len(scalars) + [VMEM] * len(arrays),
        out_specs=[VMEM] * len(outs) if several else VMEM,
        compiler_params=pltpu.CompilerParams(vmem_limit_bytes=mib * 1024 * 1024),
        cost_estimate=pl.CostEstimate(flops=flops, bytes_accessed=moved, transcendentals=0),
    )(*scalars, *arrays)


def swapped(shard, bit):
    return lax.ppermute(shard, "tp", [(i, i ^ bit) for i in range(lax.axis_size("tp"))])


def over(axis, shard, groups=None):
    return lax.all_to_all(
        shard, axis, split_axis=0, concat_axis=0, axis_index_groups=groups, tiled=True
    )


def dot(a, b, dims=(((1,), (0,)), ((), ()))):
    return lax.dot_general(a, b, dims, preferred_element_type=F32)


def pack_kernel(tok_ref, out_ref):
    turned = tok_ref[...]
    third = turned.shape[0] // 3
    packed = jnp.concatenate([turned[j * third : (j + 1) * third] for j in range(3)], axis=1)
    for z in range(out_ref.shape[0]):
        out_ref[z] = packed


def arrange_kernel(gate_ref, up_ref, gate_out_ref, up_out_ref):
    feat = gate_ref.shape[0] // (NX * NZL)
    for x in range(NX):
        for z in range(NZL):
            src, dst = (z * NX + x) * feat, (x * NZL + z) * feat
            gate_out_ref[dst : dst + feat] = gate_ref[src : src + feat]
            up_out_ref[dst : dst + feat] = up_ref[src : src + feat]


def one_hot(slot_ref, slot_total):
    n_tok = slot_ref.shape[1]
    slots = lax.broadcasted_iota(jnp.int32, (slot_total, n_tok), 0)
    hit = (slots == slot_ref[0:1, :]) | (slots == slot_ref[1:2, :])
    return jnp.where(hit, 1.0, 0.0).astype(BF16)


def dispatch_kernel(slot_ref, raw_ref, out_ref):
    n_tok = slot_ref.shape[1]
    pieces = [
        raw_ref[z, :, j * n_tok : (j + 1) * n_tok] for z in range(raw_ref.shape[0]) for j in range(3)
    ]
    raw = jnp.concatenate(pieces, axis=0)
    out_ref[...] = dot(one_hot(slot_ref, out_ref.shape[0]), raw, NT).astype(BF16)


def halves(y_ref, width):
    own = pl.multiple_of(y_ref[0] * width, width)
    other = pl.multiple_of((1 - y_ref[0]) * width, width)
    return pl.ds(own, width), pl.ds(other, width)


def forward_kernel(y_ref, rows_ref, gate_ref, up_ref, *out_refs, mine):
    width = gate_ref.shape[1] // 2
    at = halves(y_ref, width)[0 if mine else 1]
    part = out_refs[0].shape[0]
    rows = jnp.concatenate([rows_ref[x] for x in range(rows_ref.shape[0])], axis=1)
    for m, w_ref in enumerate((gate_ref, up_ref)):
        out = dot(rows, w_ref[:, at])
        for c, out_ref in enumerate(out_refs):
            out_ref[:, m * width : (m + 1) * width] = out[c * part : (c + 1) * part].astype(out_ref.dtype)


def near_kernel(keep_ref, near_ref, send_ref):
    send_ref[...] = (keep_ref[...] + near_ref[...].astype(F32)).astype(BF16)


def grad_kernel(zh_ref, keep_ref, near_ref, got_ref, hid_ref, far_ref, out_ref, *, chunk):
    rows, hid = keep_ref.shape[0], hid_ref.shape[1]
    total = keep_ref[...] + near_ref[...].astype(F32) + got_ref[...].astype(F32)
    at = slice(chunk * rows, (chunk + 1) * rows)
    own, far = hid_ref[at].astype(F32), far_ref[at].astype(F32)
    for j in range(2):
        upstream = jnp.where(zh_ref[0] == j, own, far)
        gate_pre = total[:, j * hid : (j + 1) * hid]
        up_pre = total[:, (2 + j) * hid : (3 + j) * hid]
        sig = jax.nn.sigmoid(gate_pre)
        gate_grad = upstream * up_pre * sig * (1.0 + gate_pre * (1.0 - sig))
        out_ref[:, j * hid : (j + 1) * hid] = gate_grad.astype(BF16)
        out_ref[:, (2 + j) * hid : (3 + j) * hid] = (upstream * gate_pre * sig).astype(BF16)


def backward(y_ref, grad_ref, gate_ref, up_ref, x, wide, mine):
    width = gate_ref.shape[1] // 2
    at = halves(y_ref, width)[0 if mine else 1]
    r = slice(x * wide, (x + 1) * wide)
    return dot(grad_ref[:, :width], gate_ref[r, at], NT) + dot(grad_ref[:, width:], up_ref[r, at], NT)


def backward_first_kernel(y_ref, own_ref, other_ref, gate_ref, up_ref, out_ref):
    weights = gate_ref, up_ref
    for x in range(out_ref.shape[0]):
        total = backward(y_ref, own_ref, *weights, x, out_ref.shape[2], True)
        total = total + backward(y_ref, other_ref, *weights, x, out_ref.shape[2], False)
        out_ref[x] = total.astype(BF16)


def backward_own_kernel(y_ref, own_ref, gate_ref, up_ref, out_ref):
    for x in range(out_ref.shape[0]):
        out_ref[x] = backward(y_ref, own_ref, gate_ref, up_ref, x, out_ref.shape[2], True)


def backward_last_kernel(y_ref, other_ref, gate_ref, up_ref, held_ref, first_ref, out_ref):
    rows = first_ref.shape[1]
    for x in range(out_ref.shape[0]):
        total = held_ref[x] + backward(y_ref, other_ref, gate_ref, up_ref, x, out_ref.shape[2], False)
        out_ref[x, :rows] = first_ref[x]
        out_ref[x, rows:] = total.astype(BF16)


def sum_kernel(pieces_ref, out_ref):
    total = pieces_ref[0].astype(F32)
    for x in range(1, pieces_ref.shape[0]):
        total = total + pieces_ref[x].astype(F32)
    out_ref[...] = total.astype(BF16)


def combine_kernel(slot_ref, back_ref, out_ref):
    placing = one_hot(slot_ref, back_ref.shape[0])
    part = dot(back_ref[...], placing, TN)
    half = out_ref.shape[1]
    for z in range(out_ref.shape[0]):
        low = part[2 * z * half : (2 * z + 1) * half]
        out_ref[z] = jnp.concatenate([low, part[(2 * z + 1) * half : (2 * z + 2) * half]], axis=1)


def finish_kernel(part_ref, out_ref):
    total = part_ref[0]
    for z in range(1, part_ref.shape[0]):
        total = total + part_ref[z]
    n_tok = out_ref.shape[1]
    out_ref[...] = jnp.concatenate([total[:, :n_tok], total[:, n_tok:]], axis=0).astype(BF16)


def body(tokens, routes, w_gate, w_up, hidden_grad):
    position = lax.axis_index("tp")
    y_at = jnp.bitwise_and(jnp.right_shift(position, 6), 1).reshape(1)
    zh_at = jnp.bitwise_and(jnp.right_shift(position, 5), 1).reshape(1)
    n_groups = lax.axis_size("expert")
    slot_total = hidden_grad.shape[1]
    capacity = slot_total // n_groups
    n_tok, feat = tokens.shape
    block_rows = w_gate.shape[2]
    hid = w_gate.shape[4]
    wide = NZL * feat
    shape = jax.ShapeDtypeStruct

    half = 4 * hid
    flat = [w[0, 0].reshape(block_rows, half) for w in (w_gate, w_up)]
    gate, up = call(arrange_kernel, [shape((block_rows, half), BF16)] * 2, [], flat, mib=16)

    packed = call(pack_kernel, shape((NZL, feat // 3, 3 * n_tok), BF16), [], [tokens.T])
    raw = over("tp", packed, ZL_GROUPS)

    flat_routes = routes.reshape(n_tok * 2)
    named = (flat_routes[:, None] == jnp.arange(n_groups, dtype=jnp.int32)[None, :]).astype(jnp.int32)
    before = jnp.cumsum(named, axis=0) - named
    slot_index = flat_routes * capacity + jnp.sum(before * named, axis=1)
    slot_index = slot_index.reshape(n_tok, 2).T

    outgoing = call(dispatch_kernel, shape((slot_total, wide), BF16), [], [slot_index, raw])
    arrived = over("expert", outgoing)
    hidden = hidden_grad[0]
    hidden_far = swapped(hidden, ZH_BIT)
    arrived, gate, up, hidden_far = lax.optimization_barrier((arrived, gate, up, hidden_far))
    rows = lax.all_gather(arrived, "tp", axis_index_groups=X_GROUPS, axis=0, tiled=False)

    n_flops = 2 * slot_total * block_rows * half
    part = slot_total // 2
    given = [rows, gate, up]
    send = call(
        functools.partial(forward_kernel, mine=False),
        [shape((part, half), BF16)] * 2,
        [y_at],
        given,
        n_flops,
        16,
    )
    near = [swapped(v, Y_BIT) for v in send]
    keep = call(
        functools.partial(forward_kernel, mine=True),
        [shape((part, half), F32)] * 2,
        [y_at],
        given,
        n_flops,
        16,
    )
    got = [
        swapped(call(near_kernel, shape((part, half), BF16), [], [k, n]), ZH_BIT)
        for k, n in zip(keep, near)
    ]

    def gradients(c):
        return call(
            functools.partial(grad_kernel, chunk=c),
            shape((part, half), BF16),
            [zh_at],
            [keep[c], near[c], got[c], hidden, hidden_far],
        )

    own = gradients(0)
    first = call(
        backward_first_kernel,
        shape((NX, part, wide), BF16),
        [y_at],
        [own, swapped(own, Y_BIT), gate, up],
        n_flops,
        16,
    )
    own = gradients(1)
    other = swapped(own, Y_BIT)
    held = call(
        backward_own_kernel, shape((NX, part, wide), F32), [y_at], [own, gate, up], n_flops // 2, 16
    )
    pieces = call(
        backward_last_kernel,
        shape((NX, slot_total, wide), BF16),
        [y_at],
        [other, gate, up, held, first],
        n_flops // 2,
        16,
    )
    pieces = over("tp", pieces, X_GROUPS)
    summed = call(sum_kernel, shape((slot_total, wide), BF16), [], [pieces])
    returned = over("expert", summed)

    shares = call(combine_kernel, shape((NZL, feat // 2, 2 * n_tok), F32), [], [slot_index, returned])
    shares = over("tp", shares, ZL_GROUPS)
    total = call(finish_kernel, shape((feat, n_tok), BF16), [], [shares])
    return total.T


def solution(mesh):
    placed = (
        P("expert", "tp"),
        P("expert", None),
        P("expert", "tp", None, None, None),
        P("expert", "tp", None, None, None),
        P("expert", None, "tp"),
    )
    return jax.shard_map(
        body, mesh=mesh, in_specs=placed, out_specs=P("expert", "tp"), check_vma=False
    )
```

```python
import functools

import jax
import jax.numpy as jnp
from jax import lax
from jax.experimental import pallas as pl
from jax.experimental.pallas import tpu as pltpu
from jax.sharding import PartitionSpec as P

NK, NM = 4, 8
FEW, TILE = 16, 128


def groups(bits, count=128):
    mask = sum(1 << b for b in bits)
    spread = [sum(((k >> i) & 1) << b for i, b in enumerate(bits)) for k in range(1 << len(bits))]
    return [[base | v for v in spread] for base in range(count) if not base & mask]


M_GROUPS, K_GROUPS, ZH_GROUPS = groups((0, 1, 2)), groups((3, 4)), groups((5,))
Y_BIT = 64
F32, BF16 = jnp.float32, jnp.bfloat16
NT = (((1,), (1,)), ((), ()))
TN = (((0,), (0,)), ((), ()))
VMEM = pl.BlockSpec(memory_space=pltpu.VMEM)
SMEM = pl.BlockSpec(memory_space=pltpu.SMEM)


def call(kernel, outs, scalars, arrays, flops=0, mib=6):
    several = isinstance(outs, (tuple, list))
    moved = sum(v.size * v.dtype.itemsize for v in [*arrays, *(outs if several else [outs])])
    return pl.pallas_call(
        kernel,
        out_shape=outs,
        in_specs=[SMEM] * len(scalars) + [VMEM] * len(arrays),
        out_specs=[VMEM] * len(outs) if several else VMEM,
        compiler_params=pltpu.CompilerParams(vmem_limit_bytes=mib * 1024 * 1024),
        cost_estimate=pl.CostEstimate(flops=flops, bytes_accessed=moved, transcendentals=0),
    )(*scalars, *arrays)


def swapped(shard, bit):
    return lax.ppermute(shard, "tp", [(i, i ^ bit) for i in range(lax.axis_size("tp"))])


def over(axis, shard, groups=None):
    return lax.all_to_all(
        shard, axis, split_axis=0, concat_axis=0, axis_index_groups=groups, tiled=True
    )


def dot(a, b, dims=(((1,), (0,)), ((), ()))):
    return lax.dot_general(a, b, dims, preferred_element_type=F32)


def pack_kernel(tok_ref, out_ref):
    turned = tok_ref[...]
    third = turned.shape[0] // 3
    packed = jnp.concatenate([turned[j * third : (j + 1) * third] for j in range(3)], axis=1)
    for z in range(out_ref.shape[0]):
        out_ref[z] = packed


def arrange_kernel(gate_ref, up_ref, gate_out_ref, up_out_ref):
    feat = gate_ref.shape[0] // (NM * NK)
    for m in range(NM):
        for k in range(NK):
            src, dst = (k * NM + m) * feat, (m * NK + k) * feat
            gate_out_ref[dst : dst + feat] = gate_ref[src : src + feat]
            up_out_ref[dst : dst + feat] = up_ref[src : src + feat]


def one_hot(slot_ref, half):
    shape = (TILE, slot_ref.shape[1])
    row = lax.broadcasted_iota(jnp.int32, shape, 0)
    slots = jnp.right_shift(row, 4) * (2 * FEW) + half * FEW + jnp.bitwise_and(row, FEW - 1)
    hit = (slots == slot_ref[0:1, :]) | (slots == slot_ref[1:2, :])
    return jnp.where(hit, 1.0, 0.0).astype(BF16)


def dispatch_kernel(slot_ref, raw_ref, out_ref):
    n_tok = slot_ref.shape[1]
    pieces = [
        raw_ref[k, :, j * n_tok : (j + 1) * n_tok] for k in range(raw_ref.shape[0]) for j in range(3)
    ]
    raw = jnp.concatenate(pieces, axis=0)
    out = [dot(one_hot(slot_ref, h), raw, NT) for h in range(2)]
    out_ref[...] = jnp.concatenate(out, axis=1).astype(BF16)


def copies_kernel(in_ref, out_ref):
    for m in range(out_ref.shape[0]):
        out_ref[m] = in_ref[...]


def halves(y_ref, width):
    own = pl.multiple_of(y_ref[0] * width, width)
    other = pl.multiple_of((1 - y_ref[0]) * width, width)
    return pl.ds(own, width), pl.ds(other, width)


def forward_kernel(y_ref, rows_ref, gate_ref, up_ref, out_ref, *, mine):
    width = gate_ref.shape[1] // 2
    at = halves(y_ref, width)[0 if mine else 1]
    wide = rows_ref.shape[2] // 2
    rows = [
        jnp.concatenate([rows_ref[m, :, h * wide : (h + 1) * wide] for m in range(NM)], axis=1)
        for h in range(2)
    ]
    rows = jnp.concatenate(rows, axis=0)
    for m, w_ref in enumerate((gate_ref, up_ref)):
        out_ref[:, m * width : (m + 1) * width] = dot(rows, w_ref[:, at]).astype(out_ref.dtype)


def near_kernel(keep_ref, near_ref, hid_ref, send_ref):
    width = keep_ref.shape[1]
    send_ref[:, :width] = (keep_ref[...] + near_ref[...].astype(F32)).astype(BF16)
    for h in range(2):
        for source in range(TILE // FEW):
            src, dst = (2 * source + h) * FEW, h * TILE + source * FEW
            send_ref[dst : dst + FEW, width:] = hid_ref[src : src + FEW]


def grad_kernel(zh_ref, keep_ref, near_ref, both_ref, out_ref):
    width = keep_ref.shape[1]
    hid = width // 4
    total = keep_ref[...] + near_ref[...].astype(F32)
    total = total + both_ref[1 - zh_ref[0], :, :width].astype(F32)
    for j in range(2):
        upstream = both_ref[j, :, width:].astype(F32)
        gate_pre = total[:, j * hid : (j + 1) * hid]
        up_pre = total[:, (2 + j) * hid : (3 + j) * hid]
        sig = jax.nn.sigmoid(gate_pre)
        gate_grad = upstream * up_pre * sig * (1.0 + gate_pre * (1.0 - sig))
        out_ref[:, j * hid : (j + 1) * hid] = gate_grad.astype(BF16)
        out_ref[:, (2 + j) * hid : (3 + j) * hid] = (upstream * gate_pre * sig).astype(BF16)


def backward(y_ref, grad_ref, gate_ref, up_ref, pair, mine):
    width = gate_ref.shape[1] // 2
    at = halves(y_ref, width)[0 if mine else 1]
    wide = 2 * (gate_ref.shape[0] // NM)
    r = slice(pair * wide, (pair + 1) * wide)
    return dot(grad_ref[:, :width], gate_ref[r, at], NT) + dot(grad_ref[:, width:], up_ref[r, at], NT)


def backward_own_kernel(y_ref, grad_ref, gate_ref, up_ref, out_ref):
    for pair in range(NM // 2):
        out_ref[pair] = backward(y_ref, grad_ref, gate_ref, up_ref, pair, True)


def backward_other_kernel(y_ref, grad_ref, gate_ref, up_ref, held_ref, out_ref):
    wide = out_ref.shape[2] // 2
    for pair in range(NM // 2):
        total = held_ref[pair] + backward(y_ref, grad_ref, gate_ref, up_ref, pair, False)
        total = total.astype(BF16)
        for j in range(2):
            piece = [total[h * TILE : (h + 1) * TILE, j * wide : (j + 1) * wide] for h in range(2)]
            out_ref[2 * pair + j] = jnp.concatenate(piece, axis=1)


def sum_kernel(pieces_ref, out_ref):
    total = pieces_ref[0].astype(F32)
    for m in range(1, pieces_ref.shape[0]):
        total = total + pieces_ref[m].astype(F32)
    out_ref[...] = total.astype(BF16)


def combine_kernel(slot_ref, back_ref, out_ref):
    wide = back_ref.shape[1] // 2
    back = back_ref[...]
    part = dot(back, one_hot(slot_ref, 0), TN)[:wide] + dot(back, one_hot(slot_ref, 1), TN)[wide:]
    rows = out_ref.shape[1]
    for k in range(out_ref.shape[0]):
        low = part[2 * k * rows : (2 * k + 1) * rows]
        out_ref[k] = jnp.concatenate([low, part[(2 * k + 1) * rows : (2 * k + 2) * rows]], axis=1)


def finish_kernel(part_ref, out_ref):
    total = part_ref[0]
    for z in range(1, part_ref.shape[0]):
        total = total + part_ref[z]
    n_tok = out_ref.shape[1]
    out_ref[...] = jnp.concatenate([total[:, :n_tok], total[:, n_tok:]], axis=0).astype(BF16)


def body(tokens, routes, w_gate, w_up, hidden_grad):
    position = lax.axis_index("tp")
    y_at = jnp.bitwise_and(jnp.right_shift(position, 6), 1).reshape(1)
    zh_at = jnp.bitwise_and(jnp.right_shift(position, 5), 1).reshape(1)
    n_groups = lax.axis_size("expert")
    slot_total = hidden_grad.shape[1]
    capacity = slot_total // n_groups
    n_tok, feat = tokens.shape
    block_rows = w_gate.shape[2]
    hid = w_gate.shape[4]
    wide = NK * feat
    half = 4 * hid
    shape = jax.ShapeDtypeStruct

    flat = [w[0, 0].reshape(block_rows, half) for w in (w_gate, w_up)]
    gate, up = call(arrange_kernel, [shape((block_rows, half), BF16)] * 2, [], flat, mib=16)

    packed = call(pack_kernel, shape((NK, feat // 3, 3 * n_tok), BF16), [], [tokens.T])
    raw = over("tp", packed, K_GROUPS)

    flat_routes = routes.reshape(n_tok * 2)
    named = (flat_routes[:, None] == jnp.arange(n_groups, dtype=jnp.int32)[None, :]).astype(jnp.int32)
    before = jnp.cumsum(named, axis=0) - named
    slot_index = flat_routes * capacity + jnp.sum(before * named, axis=1)
    slot_index = slot_index.reshape(n_tok, 2).T

    outgoing = call(dispatch_kernel, shape((TILE, 2 * wide), BF16), [], [slot_index, raw])
    arrived = over("expert", outgoing)
    copies = call(copies_kernel, shape((NM, TILE, 2 * wide), BF16), [], [arrived])
    rows = over("tp", copies, M_GROUPS)

    n_flops = 2 * slot_total * block_rows * half
    given = [rows, gate, up]
    send = call(
        functools.partial(forward_kernel, mine=False),
        shape((slot_total, half), BF16),
        [y_at],
        given,
        n_flops,
        16,
    )
    keep = call(
        functools.partial(forward_kernel, mine=True),
        shape((slot_total, half), F32),
        [y_at],
        given,
        n_flops,
        16,
    )
    near = swapped(send, Y_BIT)
    send = call(
        near_kernel, shape((slot_total, half + hid), BF16), [], [keep, near, hidden_grad[0]]
    )
    both = lax.all_gather(send, "tp", axis_index_groups=ZH_GROUPS, axis=0, tiled=False)

    grads = call(grad_kernel, shape((slot_total, half), BF16), [zh_at], [keep, near, both])
    other = swapped(grads, Y_BIT)
    held = call(
        backward_own_kernel,
        shape((NM // 2, slot_total, 2 * wide), F32),
        [y_at],
        [grads, gate, up],
        n_flops,
        16,
    )
    pieces = call(
        backward_other_kernel,
        shape((NM, TILE, 2 * wide), BF16),
        [y_at],
        [other, gate, up, held],
        n_flops,
        16,
    )
    pieces = over("tp", pieces, M_GROUPS)
    summed = call(sum_kernel, shape((TILE, 2 * wide), BF16), [], [pieces])
    returned = over("expert", summed)

    part = call(combine_kernel, shape((NK, feat // 2, 2 * n_tok), F32), [], [slot_index, returned])
    part = over("tp", part, K_GROUPS)
    total = call(finish_kernel, shape((feat, n_tok), BF16), [], [part])
    return total.T


def solution(mesh):
    placed = (
        P("expert", "tp"),
        P("expert", None),
        P("expert", "tp", None, None, None),
        P("expert", "tp", None, None, None),
        P("expert", None, "tp"),
    )
    return jax.shard_map(
        body, mesh=mesh, in_specs=placed, out_specs=P("expert", "tp"), check_vma=False
    )
```

```python
import functools

import jax
import jax.numpy as jnp
from jax import lax
from jax.experimental import pallas as pl
from jax.experimental.pallas import tpu as pltpu
from jax.sharding import PartitionSpec as P

NK, NM = 4, 8
FEW, TILE = 16, 128


def groups(bits, count=128):
    mask = sum(1 << b for b in bits)
    spread = [sum(((k >> i) & 1) << b for i, b in enumerate(bits)) for k in range(1 << len(bits))]
    return [[base | v for v in spread] for base in range(count) if not base & mask]


M_GROUPS, K_GROUPS, ZH_GROUPS = groups((0, 1, 2)), groups((3, 4)), groups((5,))
Y_BIT, ZH_BIT = 64, 32
F32, BF16 = jnp.float32, jnp.bfloat16
NT = (((1,), (1,)), ((), ()))
TN = (((0,), (0,)), ((), ()))
VMEM = pl.BlockSpec(memory_space=pltpu.VMEM)
SMEM = pl.BlockSpec(memory_space=pltpu.SMEM)


def call(kernel, outs, scalars, arrays, flops=0, mib=6):
    several = isinstance(outs, (tuple, list))
    moved = sum(v.size * v.dtype.itemsize for v in [*arrays, *(outs if several else [outs])])
    return pl.pallas_call(
        kernel,
        out_shape=outs,
        in_specs=[SMEM] * len(scalars) + [VMEM] * len(arrays),
        out_specs=[VMEM] * len(outs) if several else VMEM,
        compiler_params=pltpu.CompilerParams(vmem_limit_bytes=mib * 1024 * 1024),
        cost_estimate=pl.CostEstimate(flops=flops, bytes_accessed=moved, transcendentals=0),
    )(*scalars, *arrays)


def swapped(shard, bit):
    return lax.ppermute(shard, "tp", [(i, i ^ bit) for i in range(lax.axis_size("tp"))])


def over(axis, shard, groups=None):
    return lax.all_to_all(
        shard, axis, split_axis=0, concat_axis=0, axis_index_groups=groups, tiled=True
    )


def dot(a, b, dims=(((1,), (0,)), ((), ()))):
    return lax.dot_general(a, b, dims, preferred_element_type=F32)


def pack_kernel(tok_ref, out_ref):
    turned = tok_ref[...]
    third = turned.shape[0] // 3
    packed = jnp.concatenate([turned[j * third : (j + 1) * third] for j in range(3)], axis=1)
    for z in range(out_ref.shape[0]):
        out_ref[z] = packed


def place(m, f, wide):
    pair, odd = divmod(m, 2)
    at = odd * TILE + f if f < TILE else 2 * TILE + odd * (wide - TILE) + f - TILE
    return 2 * pair * wide + at


def arrange_kernel(gate_ref, up_ref, gate_out_ref, up_out_ref):
    feat = gate_ref.shape[0] // (NM * NK)
    for m in range(NM):
        for k in range(NK):
            src, low = (k * NM + m) * feat, k * feat
            cut = min(max(TILE - low, 0), feat)
            for a, b in ((0, cut), (cut, feat)):
                if a < b:
                    dst = place(m, low + a, NK * feat)
                    gate_out_ref[dst : dst + b - a] = gate_ref[src + a : src + b]
                    up_out_ref[dst : dst + b - a] = up_ref[src + a : src + b]


def one_hot(slot_ref, half):
    shape = (TILE, slot_ref.shape[1])
    row = lax.broadcasted_iota(jnp.int32, shape, 0)
    slots = jnp.right_shift(row, 4) * (2 * FEW) + half * FEW + jnp.bitwise_and(row, FEW - 1)
    hit = (slots == slot_ref[0:1, :]) | (slots == slot_ref[1:2, :])
    return jnp.where(hit, 1.0, 0.0).astype(BF16)


def dispatch_kernel(slot_ref, raw_ref, out_ref):
    n_tok = slot_ref.shape[1]
    pieces = [
        raw_ref[k, :, j * n_tok : (j + 1) * n_tok] for k in range(raw_ref.shape[0]) for j in range(3)
    ]
    raw = jnp.concatenate(pieces, axis=0)
    swap = jnp.concatenate([raw[TILE:], raw[:TILE]], axis=0)
    out = [dot(one_hot(slot_ref, 0), raw, NT), dot(one_hot(slot_ref, 1), swap, NT)]
    out_ref[...] = jnp.concatenate(out, axis=1).astype(BF16)


def copies_kernel(in_ref, out_ref):
    for m in range(out_ref.shape[0]):
        out_ref[m] = in_ref[...]


def halves(y_ref, width):
    own = pl.multiple_of(y_ref[0] * width, width)
    other = pl.multiple_of((1 - y_ref[0]) * width, width)
    return pl.ds(own, width), pl.ds(other, width)


def forward_kernel(y_ref, rows_ref, gate_ref, up_ref, out_ref, *, mine):
    width = gate_ref.shape[1] // 2
    at = halves(y_ref, width)[0 if mine else 1]
    wide = rows_ref.shape[2] // 2
    rows = []
    for head, tail in ((slice(0, TILE), slice(TILE, wide)), (slice(2 * wide - TILE, 2 * wide), slice(wide, 2 * wide - TILE))):
        cols = []
        for m in range(0, NM, 2):
            cols += [rows_ref[m, :, head], rows_ref[m + 1, :, head]]
            cols.append(jnp.concatenate([rows_ref[m, :, tail], rows_ref[m + 1, :, tail]], axis=1))
        rows.append(jnp.concatenate(cols, axis=1))
    rows = jnp.concatenate(rows, axis=0)
    for m, w_ref in enumerate((gate_ref, up_ref)):
        out_ref[:, m * width : (m + 1) * width] = dot(rows, w_ref[:, at]).astype(out_ref.dtype)


def near_kernel(keep_ref, near_ref, send_ref):
    send_ref[...] = (keep_ref[...] + near_ref[...].astype(F32)).astype(BF16)


def slot_order(ref):
    starts = [(2 * source + h) * FEW for h in range(2) for source in range(TILE // FEW)]
    return jnp.concatenate([ref[v : v + FEW] for v in starts], axis=0).astype(F32)


def grad_kernel(zh_ref, keep_ref, near_ref, both_ref, hid_ref, far_ref, out_ref):
    width = keep_ref.shape[1]
    hid = width // 4
    total = keep_ref[...] + near_ref[...].astype(F32) + both_ref[1 - zh_ref[0]].astype(F32)
    own, far = slot_order(hid_ref), slot_order(far_ref)
    for j in range(2):
        upstream = jnp.where(zh_ref[0] == j, own, far)
        gate_pre = total[:, j * hid : (j + 1) * hid]
        up_pre = total[:, (2 + j) * hid : (3 + j) * hid]
        sig = jax.nn.sigmoid(gate_pre)
        gate_grad = upstream * up_pre * sig * (1.0 + gate_pre * (1.0 - sig))
        out_ref[:, j * hid : (j + 1) * hid] = gate_grad.astype(BF16)
        out_ref[:, (2 + j) * hid : (3 + j) * hid] = (upstream * gate_pre * sig).astype(BF16)


def backward(y_ref, grad_ref, gate_ref, up_ref, pair, mine):
    width = gate_ref.shape[1] // 2
    at = halves(y_ref, width)[0 if mine else 1]
    wide = 2 * (gate_ref.shape[0] // NM)
    r = slice(pair * wide, (pair + 1) * wide)
    return dot(grad_ref[:, :width], gate_ref[r, at], NT) + dot(grad_ref[:, width:], up_ref[r, at], NT)


def backward_own_kernel(y_ref, grad_ref, gate_ref, up_ref, out_ref):
    for pair in range(NM // 2):
        out_ref[pair] = backward(y_ref, grad_ref, gate_ref, up_ref, pair, True)


def backward_other_kernel(y_ref, grad_ref, gate_ref, up_ref, held_ref, out_ref):
    wide = out_ref.shape[2] // 2
    for pair in range(NM // 2):
        total = held_ref[pair] + backward(y_ref, grad_ref, gate_ref, up_ref, pair, False)
        total = total.astype(BF16)
        tail = wide - TILE
        for j in range(2):
            head, at = slice(j * TILE, (j + 1) * TILE), 2 * TILE + j * tail
            out_ref[2 * pair + j, :, :TILE] = total[:TILE, head]
            out_ref[2 * pair + j, :, 2 * wide - TILE :] = total[TILE:, head]
            mixed = [total[:TILE, at : at + tail], total[TILE:, at : at + tail]]
            out_ref[2 * pair + j, :, TILE : 2 * wide - TILE] = jnp.concatenate(mixed, axis=1)


def sum_kernel(pieces_ref, out_ref):
    total = pieces_ref[0].astype(F32)
    for m in range(1, pieces_ref.shape[0]):
        total = total + pieces_ref[m].astype(F32)
    out_ref[...] = total.astype(BF16)


def combine_kernel(slot_ref, back_ref, out_ref):
    wide = back_ref.shape[1] // 2
    back = back_ref[...]
    last = dot(back, one_hot(slot_ref, 1), TN)
    last = jnp.concatenate([last[2 * wide - TILE :], last[wide : 2 * wide - TILE]], axis=0)
    part = dot(back, one_hot(slot_ref, 0), TN)[:wide] + last
    rows = out_ref.shape[1]
    for k in range(out_ref.shape[0]):
        low = part[2 * k * rows : (2 * k + 1) * rows]
        out_ref[k] = jnp.concatenate([low, part[(2 * k + 1) * rows : (2 * k + 2) * rows]], axis=1)


def finish_kernel(part_ref, out_ref):
    total = part_ref[0]
    for z in range(1, part_ref.shape[0]):
        total = total + part_ref[z]
    n_tok = out_ref.shape[1]
    out_ref[...] = jnp.concatenate([total[:, :n_tok], total[:, n_tok:]], axis=0).astype(BF16)


def body(tokens, routes, w_gate, w_up, hidden_grad):
    position = lax.axis_index("tp")
    y_at = jnp.bitwise_and(jnp.right_shift(position, 6), 1).reshape(1)
    zh_at = jnp.bitwise_and(jnp.right_shift(position, 5), 1).reshape(1)
    n_groups = lax.axis_size("expert")
    slot_total = hidden_grad.shape[1]
    capacity = slot_total // n_groups
    n_tok, feat = tokens.shape
    block_rows = w_gate.shape[2]
    hid = w_gate.shape[4]
    wide = NK * feat
    half = 4 * hid
    shape = jax.ShapeDtypeStruct

    flat = [w[0, 0].reshape(block_rows, half) for w in (w_gate, w_up)]
    gate, up = call(arrange_kernel, [shape((block_rows, half), BF16)] * 2, [], flat, mib=16)

    packed = call(pack_kernel, shape((NK, feat // 3, 3 * n_tok), BF16), [], [tokens.T])
    raw = over("tp", packed, K_GROUPS)

    flat_routes = routes.reshape(n_tok * 2)
    named = (flat_routes[:, None] == jnp.arange(n_groups, dtype=jnp.int32)[None, :]).astype(jnp.int32)
    before = jnp.cumsum(named, axis=0) - named
    slot_index = flat_routes * capacity + jnp.sum(before * named, axis=1)
    slot_index = slot_index.reshape(n_tok, 2).T

    outgoing = call(dispatch_kernel, shape((TILE, 2 * wide), BF16), [], [slot_index, raw])
    arrived = over("expert", outgoing)
    copies = call(copies_kernel, shape((NM, TILE, 2 * wide), BF16), [], [arrived])
    rows = over("tp", copies, M_GROUPS)
    hidden = hidden_grad[0]
    hidden_far = swapped(hidden, ZH_BIT)
    rows, hidden_far = lax.optimization_barrier((rows, hidden_far))

    n_flops = 2 * slot_total * block_rows * half
    given = [rows, gate, up]
    send = call(
        functools.partial(forward_kernel, mine=False),
        shape((slot_total, half), BF16),
        [y_at],
        given,
        n_flops,
        16,
    )
    keep = call(
        functools.partial(forward_kernel, mine=True),
        shape((slot_total, half), F32),
        [y_at],
        given,
        n_flops,
        16,
    )
    near = swapped(send, Y_BIT)
    send = call(near_kernel, shape((slot_total, half), BF16), [], [keep, near])
    both = lax.all_gather(send, "tp", axis_index_groups=ZH_GROUPS, axis=0, tiled=False)

    grads = call(grad_kernel, shape((slot_total, half), BF16), [zh_at], [keep, near, both, hidden, hidden_far])
    other = swapped(grads, Y_BIT)
    held = call(
        backward_own_kernel,
        shape((NM // 2, slot_total, 2 * wide), F32),
        [y_at],
        [grads, gate, up],
        n_flops,
        16,
    )
    pieces = call(
        backward_other_kernel,
        shape((NM, TILE, 2 * wide), BF16),
        [y_at],
        [other, gate, up, held],
        n_flops,
        16,
    )
    pieces = over("tp", pieces, M_GROUPS)
    summed = call(sum_kernel, shape((TILE, 2 * wide), BF16), [], [pieces])
    returned = over("expert", summed)

    part = call(combine_kernel, shape((NK, feat // 2, 2 * n_tok), F32), [], [slot_index, returned])
    part = over("tp", part, K_GROUPS)
    total = call(finish_kernel, shape((feat, n_tok), BF16), [], [part])
    return total.T


def solution(mesh):
    placed = (
        P("expert", "tp"),
        P("expert", None),
        P("expert", "tp", None, None, None),
        P("expert", "tp", None, None, None),
        P("expert", None, "tp"),
    )
    return jax.shard_map(
        body, mesh=mesh, in_specs=placed, out_specs=P("expert", "tp"), check_vma=False
    )
```

```python
import functools

import jax
import jax.numpy as jnp
from jax import lax
from jax.experimental import pallas as pl
from jax.experimental.pallas import tpu as pltpu
from jax.sharding import PartitionSpec as P

NX, NZL, NK = 4, 8, 4
ORDER = [2 * k + z0 for z0 in range(2) for k in range(NK)]
FEW, TILE = 16, 128


def groups(bits, count=128):
    mask = sum(1 << b for b in bits)
    spread = [sum(((k >> i) & 1) << b for i, b in enumerate(bits)) for k in range(1 << len(bits))]
    return [[base | v for v in spread] for base in range(count) if not base & mask]


X_GROUPS, ZL_GROUPS, ZH_GROUPS = groups((0, 1)), groups((2, 3, 4)), groups((5,))
M_GROUPS, K_GROUPS = groups((0, 1, 2)), groups((3, 4))
Y_BIT, ZH_BIT = 64, 32
F32, BF16 = jnp.float32, jnp.bfloat16
NT = (((1,), (1,)), ((), ()))
TN = (((0,), (0,)), ((), ()))
VMEM = pl.BlockSpec(memory_space=pltpu.VMEM)
SMEM = pl.BlockSpec(memory_space=pltpu.SMEM)


def call(kernel, outs, scalars, arrays, flops=0, mib=6):
    several = isinstance(outs, (tuple, list))
    moved = sum(v.size * v.dtype.itemsize for v in [*arrays, *(outs if several else [outs])])
    return pl.pallas_call(
        kernel,
        out_shape=outs,
        in_specs=[SMEM] * len(scalars) + [VMEM] * len(arrays),
        out_specs=[VMEM] * len(outs) if several else VMEM,
        compiler_params=pltpu.CompilerParams(vmem_limit_bytes=mib * 1024 * 1024),
        cost_estimate=pl.CostEstimate(flops=flops, bytes_accessed=moved, transcendentals=0),
    )(*scalars, *arrays)


def swapped(shard, bit):
    return lax.ppermute(shard, "tp", [(i, i ^ bit) for i in range(lax.axis_size("tp"))])


def over(axis, shard, groups=None):
    return lax.all_to_all(
        shard, axis, split_axis=0, concat_axis=0, axis_index_groups=groups, tiled=True
    )


def dot(a, b, dims=(((1,), (0,)), ((), ()))):
    return lax.dot_general(a, b, dims, preferred_element_type=F32)


def pack_kernel(tok_ref, out_ref):
    turned = tok_ref[...]
    third = turned.shape[0] // 3
    packed = jnp.concatenate([turned[j * third : (j + 1) * third] for j in range(3)], axis=1)
    for z in range(out_ref.shape[0]):
        out_ref[z] = packed


def arrange_kernel(in_ref, out_ref):
    feat = in_ref.shape[0] // (NX * NZL)
    for x in range(NX):
        for at, z in enumerate(ORDER):
            src, dst = (z * NX + x) * feat, (x * NZL + at) * feat
            out_ref[dst : dst + feat] = in_ref[src : src + feat]


def one_hot(slot_ref, slots):
    hit = (slots == slot_ref[0:1, :]) | (slots == slot_ref[1:2, :])
    return jnp.where(hit, 1.0, 0.0).astype(BF16)


def dispatch_kernel(slot_ref, raw_ref, out_ref):
    n_tok = slot_ref.shape[1]
    pieces = [
        raw_ref[z, :, j * n_tok : (j + 1) * n_tok] for z in ORDER for j in range(3)
    ]
    raw = jnp.concatenate(pieces, axis=0)
    slots = lax.broadcasted_iota(jnp.int32, (out_ref.shape[0], n_tok), 0)
    out_ref[...] = dot(one_hot(slot_ref, slots), raw, NT).astype(BF16)


def halves(y_ref, width):
    own = pl.multiple_of(y_ref[0] * width, width)
    other = pl.multiple_of((1 - y_ref[0]) * width, width)
    return pl.ds(own, width), pl.ds(other, width)


def forward_kernel(y_ref, rows_ref, gate_ref, up_ref, out_ref, *, mine):
    width = gate_ref.shape[1] // 2
    at = halves(y_ref, width)[0 if mine else 1]
    rows = jnp.concatenate([rows_ref[x] for x in range(rows_ref.shape[0])], axis=1)
    for m, w_ref in enumerate((gate_ref, up_ref)):
        out_ref[:, m * width : (m + 1) * width] = dot(rows, w_ref[:, at]).astype(out_ref.dtype)


def near_kernel(keep_ref, near_ref, send_ref):
    send_ref[...] = (keep_ref[...] + near_ref[...].astype(F32)).astype(BF16)


def grad_kernel(zh_ref, keep_ref, near_ref, both_ref, hid_ref, far_ref, out_ref):
    width = keep_ref.shape[1]
    hid = width // 4
    total = keep_ref[...] + near_ref[...].astype(F32) + both_ref[1 - zh_ref[0]].astype(F32)
    own, far = hid_ref[...].astype(F32), far_ref[...].astype(F32)
    for j in range(2):
        upstream = jnp.where(zh_ref[0] == j, own, far)
        gate_pre = total[:, j * hid : (j + 1) * hid]
        up_pre = total[:, (2 + j) * hid : (3 + j) * hid]
        sig = jax.nn.sigmoid(gate_pre)
        gate_grad = upstream * up_pre * sig * (1.0 + gate_pre * (1.0 - sig))
        out_ref[:, j * hid : (j + 1) * hid] = gate_grad.astype(BF16)
        out_ref[:, (2 + j) * hid : (3 + j) * hid] = (upstream * gate_pre * sig).astype(BF16)


def backward(y_ref, grad_ref, gate_ref, up_ref, x, mine):
    width = gate_ref.shape[1] // 2
    at = halves(y_ref, width)[0 if mine else 1]
    wide = gate_ref.shape[0] // NX
    r = slice(x * wide, (x + 1) * wide)
    return dot(grad_ref[:, :width], gate_ref[r, at], NT) + dot(grad_ref[:, width:], up_ref[r, at], NT)


def backward_own_kernel(y_ref, grad_ref, gate_ref, up_ref, out_ref):
    for x in range(NX):
        out_ref[x] = backward(y_ref, grad_ref, gate_ref, up_ref, x, True)


def backward_other_kernel(y_ref, grad_ref, gate_ref, up_ref, held_ref, out_ref):
    wide = out_ref.shape[2] // 2
    for x in range(NX):
        total = held_ref[x] + backward(y_ref, grad_ref, gate_ref, up_ref, x, False)
        total = total.astype(BF16)
        part = []
        for h in range(2):
            starts = [(2 * e + h) * FEW for e in range(TILE // FEW)]
            part.append(jnp.concatenate([total[v : v + FEW] for v in starts], axis=0))
        for z0 in range(2):
            at = slice(z0 * wide, (z0 + 1) * wide)
            out_ref[z0 * NX + x] = jnp.concatenate([part[0][:, at], part[1][:, at]], axis=1)


def sum_kernel(pieces_ref, out_ref):
    total = pieces_ref[0].astype(F32)
    for x in range(1, pieces_ref.shape[0]):
        total = total + pieces_ref[x].astype(F32)
    out_ref[...] = total.astype(BF16)


def returned_rows(slot_ref, half):
    row = lax.broadcasted_iota(jnp.int32, (TILE, slot_ref.shape[1]), 0)
    return jnp.right_shift(row, 4) * (2 * FEW) + half * FEW + jnp.bitwise_and(row, FEW - 1)


def combine_kernel(slot_ref, back_ref, out_ref):
    wide = back_ref.shape[1] // 2
    back = back_ref[...]
    part = [dot(back, one_hot(slot_ref, returned_rows(slot_ref, h)), TN) for h in range(2)]
    part = part[0][:wide] + part[1][wide:]
    rows = out_ref.shape[1]
    for k in range(out_ref.shape[0]):
        low = part[2 * k * rows : (2 * k + 1) * rows]
        out_ref[k] = jnp.concatenate([low, part[(2 * k + 1) * rows : (2 * k + 2) * rows]], axis=1)


def finish_kernel(part_ref, out_ref):
    total = part_ref[0]
    for z in range(1, part_ref.shape[0]):
        total = total + part_ref[z]
    n_tok = out_ref.shape[1]
    out_ref[...] = jnp.concatenate([total[:, :n_tok], total[:, n_tok:]], axis=0).astype(BF16)


def body(tokens, routes, w_gate, w_up, hidden_grad):
    position = lax.axis_index("tp")
    y_at = jnp.bitwise_and(jnp.right_shift(position, 6), 1).reshape(1)
    zh_at = jnp.bitwise_and(jnp.right_shift(position, 5), 1).reshape(1)
    n_groups = lax.axis_size("expert")
    slot_total = hidden_grad.shape[1]
    capacity = slot_total // n_groups
    n_tok, feat = tokens.shape
    block_rows = w_gate.shape[2]
    hid = w_gate.shape[4]
    wide = NZL * feat
    shape = jax.ShapeDtypeStruct

    half = 4 * hid
    gate, up = [
        call(arrange_kernel, shape((block_rows, half), BF16), [], [w[0, 0].reshape(block_rows, half)])
        for w in (w_gate, w_up)
    ]

    packed = call(pack_kernel, shape((NZL, feat // 3, 3 * n_tok), BF16), [], [tokens.T])
    raw = over("tp", packed, ZL_GROUPS)

    flat_routes = routes.reshape(n_tok * 2)
    named = (flat_routes[:, None] == jnp.arange(n_groups, dtype=jnp.int32)[None, :]).astype(jnp.int32)
    before = jnp.cumsum(named, axis=0) - named
    slot_index = flat_routes * capacity + jnp.sum(before * named, axis=1)
    slot_index = slot_index.reshape(n_tok, 2).T

    outgoing = call(dispatch_kernel, shape((slot_total, wide), BF16), [], [slot_index, raw])
    arrived = over("expert", outgoing)
    hidden = hidden_grad[0]
    hidden_far = swapped(hidden, ZH_BIT)
    arrived, gate, up = lax.optimization_barrier((arrived, gate, up))
    rows = lax.all_gather(arrived, "tp", axis_index_groups=X_GROUPS, axis=0, tiled=False)
    rows, hidden_far = lax.optimization_barrier((rows, hidden_far))

    n_flops = 2 * slot_total * block_rows * half
    given = [rows, gate, up]
    send = call(
        functools.partial(forward_kernel, mine=False),
        shape((slot_total, half), BF16),
        [y_at],
        given,
        n_flops,
        16,
    )
    keep = call(
        functools.partial(forward_kernel, mine=True),
        shape((slot_total, half), F32),
        [y_at],
        given,
        n_flops,
        16,
    )
    near = swapped(send, Y_BIT)
    send = call(near_kernel, shape((slot_total, half), BF16), [], [keep, near])
    both = lax.all_gather(send, "tp", axis_index_groups=ZH_GROUPS, axis=0, tiled=False)

    grads = call(
        grad_kernel,
        shape((slot_total, half), BF16),
        [zh_at],
        [keep, near, both, hidden, hidden_far],
    )
    other = swapped(grads, Y_BIT)
    held = call(
        backward_own_kernel,
        shape((NX, slot_total, wide), F32),
        [y_at],
        [grads, gate, up],
        n_flops,
        16,
    )
    pieces = call(
        backward_other_kernel,
        shape((2 * NX, TILE, wide), BF16),
        [y_at],
        [other, gate, up, held],
        n_flops,
        16,
    )
    pieces = over("tp", pieces, M_GROUPS)
    summed = call(sum_kernel, shape((TILE, wide), BF16), [], [pieces])
    returned = over("expert", summed)

    part = call(combine_kernel, shape((NK, feat // 2, 2 * n_tok), F32), [], [slot_index, returned])
    part = over("tp", part, K_GROUPS)
    total = call(finish_kernel, shape((feat, n_tok), BF16), [], [part])
    return total.T


def solution(mesh):
    placed = (
        P("expert", "tp"),
        P("expert", None),
        P("expert", "tp", None, None, None),
        P("expert", "tp", None, None, None),
        P("expert", None, "tp"),
    )
    return jax.shard_map(
        body, mesh=mesh, in_specs=placed, out_specs=P("expert", "tp"), check_vma=False
    )
```

```python
import functools

import jax
import jax.numpy as jnp
from jax import lax
from jax.experimental import pallas as pl
from jax.experimental.pallas import tpu as pltpu
from jax.sharding import PartitionSpec as P

NX, NZL, NK = 4, 8, 4
ORDER = [2 * k + z0 for z0 in range(2) for k in range(NK)]
FEW, TILE = 16, 128


def groups(bits, count=128):
    mask = sum(1 << b for b in bits)
    spread = [sum(((k >> i) & 1) << b for i, b in enumerate(bits)) for k in range(1 << len(bits))]
    return [[base | v for v in spread] for base in range(count) if not base & mask]


X_GROUPS, ZL_GROUPS, ZH_GROUPS = groups((0, 1)), groups((2, 3, 4)), groups((5,))
M_GROUPS, K_GROUPS = groups((0, 1, 2)), groups((3, 4))
Y_BIT, ZH_BIT = 64, 32
F32, BF16 = jnp.float32, jnp.bfloat16
NT = (((1,), (1,)), ((), ()))
TN = (((0,), (0,)), ((), ()))
VMEM = pl.BlockSpec(memory_space=pltpu.VMEM)
SMEM = pl.BlockSpec(memory_space=pltpu.SMEM)


def call(kernel, outs, scalars, arrays, flops=0, mib=6):
    several = isinstance(outs, (tuple, list))
    moved = sum(v.size * v.dtype.itemsize for v in [*arrays, *(outs if several else [outs])])
    return pl.pallas_call(
        kernel,
        out_shape=outs,
        in_specs=[SMEM] * len(scalars) + [VMEM] * len(arrays),
        out_specs=[VMEM] * len(outs) if several else VMEM,
        compiler_params=pltpu.CompilerParams(vmem_limit_bytes=mib * 1024 * 1024),
        cost_estimate=pl.CostEstimate(flops=flops, bytes_accessed=moved, transcendentals=0),
    )(*scalars, *arrays)


def swapped(shard, bit):
    return lax.ppermute(shard, "tp", [(i, i ^ bit) for i in range(lax.axis_size("tp"))])


def over(axis, shard, groups=None):
    return lax.all_to_all(
        shard, axis, split_axis=0, concat_axis=0, axis_index_groups=groups, tiled=True
    )


def dot(a, b, dims=(((1,), (0,)), ((), ()))):
    return lax.dot_general(a, b, dims, preferred_element_type=F32)


def pack_kernel(tok_ref, out_ref):
    turned = tok_ref[...]
    third = turned.shape[0] // 3
    packed = jnp.concatenate([turned[j * third : (j + 1) * third] for j in range(3)], axis=1)
    for z in range(out_ref.shape[0]):
        out_ref[z] = packed


def arrange_kernel(in_ref, out_ref):
    feat = in_ref.shape[0] // (NX * NZL)
    for x in range(NX):
        for at, z in enumerate(ORDER):
            src, dst = (z * NX + x) * feat, (x * NZL + at) * feat
            out_ref[dst : dst + feat] = in_ref[src : src + feat]


def one_hot(slot_ref, slots):
    hit = (slots == slot_ref[0:1, :]) | (slots == slot_ref[1:2, :])
    return jnp.where(hit, 1.0, 0.0).astype(BF16)


def dispatch_kernel(slot_ref, raw_ref, out_ref):
    n_tok = slot_ref.shape[1]
    pieces = [
        raw_ref[z, :, j * n_tok : (j + 1) * n_tok] for z in ORDER for j in range(3)
    ]
    raw = jnp.concatenate(pieces, axis=0)
    slots = lax.broadcasted_iota(jnp.int32, (out_ref.shape[0], n_tok), 0)
    out_ref[...] = dot(one_hot(slot_ref, slots), raw, NT).astype(BF16)


def halves(y_ref, width):
    own = pl.multiple_of(y_ref[0] * width, width)
    other = pl.multiple_of((1 - y_ref[0]) * width, width)
    return pl.ds(own, width), pl.ds(other, width)


def forward_kernel(y_ref, rows_ref, gate_ref, up_ref, out_ref, *, mine):
    width = gate_ref.shape[1] // 2
    at = halves(y_ref, width)[0 if mine else 1]
    rows = jnp.concatenate([rows_ref[x] for x in range(rows_ref.shape[0])], axis=1)
    for m, w_ref in enumerate((gate_ref, up_ref)):
        out_ref[:, m * width : (m + 1) * width] = dot(rows, w_ref[:, at]).astype(out_ref.dtype)


def near_kernel(keep_ref, near_ref, send_ref):
    send_ref[...] = (keep_ref[...] + near_ref[...].astype(F32)).astype(BF16)


def grad_kernel(zh_ref, keep_ref, near_ref, both_ref, hid_ref, far_ref, out_ref):
    width = keep_ref.shape[1]
    hid = width // 4
    total = keep_ref[...] + near_ref[...].astype(F32) + both_ref[1 - zh_ref[0]].astype(F32)
    own, far = hid_ref[...].astype(F32), far_ref[...].astype(F32)
    for j in range(2):
        upstream = jnp.where(zh_ref[0] == j, own, far)
        gate_pre = total[:, j * hid : (j + 1) * hid]
        up_pre = total[:, (2 + j) * hid : (3 + j) * hid]
        sig = jax.nn.sigmoid(gate_pre)
        gate_grad = upstream * up_pre * sig * (1.0 + gate_pre * (1.0 - sig))
        out_ref[:, j * hid : (j + 1) * hid] = gate_grad.astype(BF16)
        out_ref[:, (2 + j) * hid : (3 + j) * hid] = (upstream * gate_pre * sig).astype(BF16)


def backward(y_ref, grad_ref, gate_ref, up_ref, x, mine):
    width = gate_ref.shape[1] // 2
    at = halves(y_ref, width)[0 if mine else 1]
    wide = gate_ref.shape[0] // NX
    r = slice(x * wide, (x + 1) * wide)
    return dot(grad_ref[:, :width], gate_ref[r, at], NT) + dot(grad_ref[:, width:], up_ref[r, at], NT)


def backward_own_kernel(y_ref, grad_ref, gate_ref, up_ref, out_ref):
    for x in range(NX):
        out_ref[x] = backward(y_ref, grad_ref, gate_ref, up_ref, x, True)


def backward_other_kernel(y_ref, grad_ref, gate_ref, up_ref, held_ref, out_ref):
    wide = out_ref.shape[2] // 2
    for x in range(NX):
        total = held_ref[x] + backward(y_ref, grad_ref, gate_ref, up_ref, x, False)
        total = total.astype(BF16)
        part = []
        for h in range(2):
            starts = [(2 * e + h) * FEW for e in range(TILE // FEW)]
            part.append(jnp.concatenate([total[v : v + FEW] for v in starts], axis=0))
        for z0 in range(2):
            at = slice(z0 * wide, (z0 + 1) * wide)
            out_ref[z0 * NX + x] = jnp.concatenate([part[0][:, at], part[1][:, at]], axis=1)


def sum_kernel(pieces_ref, out_ref):
    total = pieces_ref[0].astype(F32)
    for x in range(1, pieces_ref.shape[0]):
        total = total + pieces_ref[x].astype(F32)
    out_ref[...] = total.astype(BF16)


def returned_rows(slot_ref, half):
    row = lax.broadcasted_iota(jnp.int32, (TILE, slot_ref.shape[1]), 0)
    return jnp.right_shift(row, 4) * (2 * FEW) + half * FEW + jnp.bitwise_and(row, FEW - 1)


def combine_kernel(slot_ref, back_ref, out_ref):
    wide = back_ref.shape[1] // 2
    back = back_ref[...]
    part = [dot(back, one_hot(slot_ref, returned_rows(slot_ref, h)), TN) for h in range(2)]
    part = part[0][:wide] + part[1][wide:]
    rows = out_ref.shape[1]
    for k in range(out_ref.shape[0]):
        low = part[2 * k * rows : (2 * k + 1) * rows]
        out_ref[k] = jnp.concatenate([low, part[(2 * k + 1) * rows : (2 * k + 2) * rows]], axis=1)


def finish_kernel(part_ref, out_ref):
    total = part_ref[0]
    for z in range(1, part_ref.shape[0]):
        total = total + part_ref[z]
    n_tok = out_ref.shape[1]
    out_ref[...] = jnp.concatenate([total[:, :n_tok], total[:, n_tok:]], axis=0).astype(BF16)


def body(tokens, routes, w_gate, w_up, hidden_grad):
    position = lax.axis_index("tp")
    y_at = jnp.bitwise_and(jnp.right_shift(position, 6), 1).reshape(1)
    zh_at = jnp.bitwise_and(jnp.right_shift(position, 5), 1).reshape(1)
    n_groups = lax.axis_size("expert")
    slot_total = hidden_grad.shape[1]
    capacity = slot_total // n_groups
    n_tok, feat = tokens.shape
    block_rows = w_gate.shape[2]
    hid = w_gate.shape[4]
    wide = NZL * feat
    shape = jax.ShapeDtypeStruct

    half = 4 * hid
    gate, up = [
        call(arrange_kernel, shape((block_rows, half), BF16), [], [w[0, 0].reshape(block_rows, half)])
        for w in (w_gate, w_up)
    ]

    packed = call(pack_kernel, shape((NZL, feat // 3, 3 * n_tok), BF16), [], [tokens.T])
    raw = over("tp", packed, ZL_GROUPS)

    flat_routes = routes.reshape(n_tok * 2)
    named = (flat_routes[:, None] == jnp.arange(n_groups, dtype=jnp.int32)[None, :]).astype(jnp.int32)
    before = jnp.cumsum(named, axis=0) - named
    slot_index = flat_routes * capacity + jnp.sum(before * named, axis=1)
    slot_index = slot_index.reshape(n_tok, 2).T

    raw, gate, up, hidden = lax.optimization_barrier((raw, gate, up, hidden_grad[0]))
    outgoing = call(dispatch_kernel, shape((slot_total, wide), BF16), [], [slot_index, raw])
    arrived = over("expert", outgoing)
    hidden_far = swapped(hidden, ZH_BIT)
    rows = lax.all_gather(arrived, "tp", axis_index_groups=X_GROUPS, axis=0, tiled=False)
    rows, hidden_far = lax.optimization_barrier((rows, hidden_far))

    n_flops = 2 * slot_total * block_rows * half
    given = [rows, gate, up]
    send = call(
        functools.partial(forward_kernel, mine=False),
        shape((slot_total, half), BF16),
        [y_at],
        given,
        n_flops,
        16,
    )
    keep = call(
        functools.partial(forward_kernel, mine=True),
        shape((slot_total, half), F32),
        [y_at],
        given,
        n_flops,
        16,
    )
    near = swapped(send, Y_BIT)
    send = call(near_kernel, shape((slot_total, half), BF16), [], [keep, near])
    both = lax.all_gather(send, "tp", axis_index_groups=ZH_GROUPS, axis=0, tiled=False)

    grads = call(
        grad_kernel,
        shape((slot_total, half), BF16),
        [zh_at],
        [keep, near, both, hidden, hidden_far],
    )
    other = swapped(grads, Y_BIT)
    held = call(
        backward_own_kernel,
        shape((NX, slot_total, wide), F32),
        [y_at],
        [grads, gate, up],
        n_flops,
        16,
    )
    pieces = call(
        backward_other_kernel,
        shape((2 * NX, TILE, wide), BF16),
        [y_at],
        [other, gate, up, held],
        n_flops,
        16,
    )
    pieces = over("tp", pieces, M_GROUPS)
    summed = call(sum_kernel, shape((TILE, wide), BF16), [], [pieces])
    returned = over("expert", summed)

    part = call(combine_kernel, shape((NK, feat // 2, 2 * n_tok), F32), [], [slot_index, returned])
    part = over("tp", part, K_GROUPS)
    total = call(finish_kernel, shape((feat, n_tok), BF16), [], [part])
    return total.T


def solution(mesh):
    placed = (
        P("expert", "tp"),
        P("expert", None),
        P("expert", "tp", None, None, None),
        P("expert", "tp", None, None, None),
        P("expert", None, "tp"),
    )
    return jax.shard_map(
        body, mesh=mesh, in_specs=placed, out_specs=P("expert", "tp"), check_vma=False
    )
```

```python
import functools

import jax
import jax.numpy as jnp
from jax import lax
from jax.experimental import pallas as pl
from jax.experimental.pallas import tpu as pltpu
from jax.sharding import Mesh
from jax.sharding import PartitionSpec as P

NX, NZL, NK = 4, 8, 4
ORDER = [2 * k + z0 for z0 in range(2) for k in range(NK)]
FEW, TILE = 16, 128

AXES = ("expert", "y", "zh", "k", "z0", "x")
F32, BF16 = jnp.float32, jnp.bfloat16
NT = (((1,), (1,)), ((), ()))
TN = (((0,), (0,)), ((), ()))
VMEM = pl.BlockSpec(memory_space=pltpu.VMEM)
SMEM = pl.BlockSpec(memory_space=pltpu.SMEM)


def call(kernel, outs, scalars, arrays, flops=0, mib=6):
    several = isinstance(outs, (tuple, list))
    moved = sum(v.size * v.dtype.itemsize for v in [*arrays, *(outs if several else [outs])])
    return pl.pallas_call(
        kernel,
        out_shape=outs,
        in_specs=[SMEM] * len(scalars) + [VMEM] * len(arrays),
        out_specs=[VMEM] * len(outs) if several else VMEM,
        compiler_params=pltpu.CompilerParams(vmem_limit_bytes=mib * 1024 * 1024),
        cost_estimate=pl.CostEstimate(flops=flops, bytes_accessed=moved, transcendentals=0),
    )(*scalars, *arrays)


def swapped(shard, axis):
    return lax.ppermute(shard, axis, [(0, 1), (1, 0)])


def over(axes, shard):
    return lax.all_to_all(shard, axes, split_axis=0, concat_axis=0, tiled=True)


def gathered(axis, shard):
    return lax.all_gather(shard, axis, axis=0, tiled=False)


def dot(a, b, dims=(((1,), (0,)), ((), ()))):
    return lax.dot_general(a, b, dims, preferred_element_type=F32)


def pack_kernel(tok_ref, out_ref):
    turned = tok_ref[...]
    third = turned.shape[0] // 3
    packed = jnp.concatenate([turned[j * third : (j + 1) * third] for j in range(3)], axis=1)
    for z in range(out_ref.shape[0]):
        out_ref[z] = packed


def arrange_kernel(in_ref, out_ref):
    feat = in_ref.shape[0] // (NX * NZL)
    for x in range(NX):
        for at, z in enumerate(ORDER):
            src, dst = (z * NX + x) * feat, (x * NZL + at) * feat
            out_ref[dst : dst + feat] = in_ref[src : src + feat]


def one_hot(slot_ref, slots):
    hit = (slots == slot_ref[0:1, :]) | (slots == slot_ref[1:2, :])
    return jnp.where(hit, 1.0, 0.0).astype(BF16)


def dispatch_kernel(slot_ref, raw_ref, out_ref):
    n_tok = slot_ref.shape[1]
    pieces = [
        raw_ref[z, :, j * n_tok : (j + 1) * n_tok] for z in ORDER for j in range(3)
    ]
    raw = jnp.concatenate(pieces, axis=0)
    slots = lax.broadcasted_iota(jnp.int32, (out_ref.shape[0], n_tok), 0)
    out_ref[...] = dot(one_hot(slot_ref, slots), raw, NT).astype(BF16)


def halves(y_ref, width):
    own = pl.multiple_of(y_ref[0] * width, width)
    other = pl.multiple_of((1 - y_ref[0]) * width, width)
    return pl.ds(own, width), pl.ds(other, width)


def forward_kernel(y_ref, rows_ref, gate_ref, up_ref, out_ref, *, mine):
    width = gate_ref.shape[1] // 2
    at = halves(y_ref, width)[0 if mine else 1]
    rows = jnp.concatenate([rows_ref[x] for x in range(rows_ref.shape[0])], axis=1)
    for m, w_ref in enumerate((gate_ref, up_ref)):
        out_ref[:, m * width : (m + 1) * width] = dot(rows, w_ref[:, at]).astype(out_ref.dtype)


def near_kernel(keep_ref, near_ref, send_ref):
    send_ref[...] = (keep_ref[...] + near_ref[...].astype(F32)).astype(BF16)


def grad_kernel(zh_ref, keep_ref, near_ref, both_ref, hid_ref, far_ref, out_ref):
    width = keep_ref.shape[1]
    hid = width // 4
    total = keep_ref[...] + near_ref[...].astype(F32) + both_ref[1 - zh_ref[0]].astype(F32)
    own, far = hid_ref[...].astype(F32), far_ref[...].astype(F32)
    for j in range(2):
        upstream = jnp.where(zh_ref[0] == j, own, far)
        gate_pre = total[:, j * hid : (j + 1) * hid]
        up_pre = total[:, (2 + j) * hid : (3 + j) * hid]
        sig = jax.nn.sigmoid(gate_pre)
        gate_grad = upstream * up_pre * sig * (1.0 + gate_pre * (1.0 - sig))
        out_ref[:, j * hid : (j + 1) * hid] = gate_grad.astype(BF16)
        out_ref[:, (2 + j) * hid : (3 + j) * hid] = (upstream * gate_pre * sig).astype(BF16)


def backward(y_ref, grad_ref, gate_ref, up_ref, x, mine):
    width = gate_ref.shape[1] // 2
    at = halves(y_ref, width)[0 if mine else 1]
    wide = gate_ref.shape[0] // NX
    r = slice(x * wide, (x + 1) * wide)
    return dot(grad_ref[:, :width], gate_ref[r, at], NT) + dot(grad_ref[:, width:], up_ref[r, at], NT)


def backward_own_kernel(y_ref, grad_ref, gate_ref, up_ref, out_ref):
    for x in range(NX):
        out_ref[x] = backward(y_ref, grad_ref, gate_ref, up_ref, x, True)


def backward_other_kernel(y_ref, grad_ref, gate_ref, up_ref, held_ref, out_ref):
    wide = out_ref.shape[2] // 2
    for x in range(NX):
        total = held_ref[x] + backward(y_ref, grad_ref, gate_ref, up_ref, x, False)
        total = total.astype(BF16)
        part = []
        for h in range(2):
            starts = [(2 * e + h) * FEW for e in range(TILE // FEW)]
            part.append(jnp.concatenate([total[v : v + FEW] for v in starts], axis=0))
        for z0 in range(2):
            at = slice(z0 * wide, (z0 + 1) * wide)
            out_ref[z0 * NX + x] = jnp.concatenate([part[0][:, at], part[1][:, at]], axis=1)


def sum_kernel(pieces_ref, out_ref):
    total = pieces_ref[0].astype(F32)
    for m in range(1, pieces_ref.shape[0]):
        total = total + pieces_ref[m].astype(F32)
    total = total.astype(BF16)
    wide = total.shape[1] // 2
    feat = wide // NK
    for k in range(NK):
        part = [total[:, h * wide + k * feat : h * wide + (k + 1) * feat] for h in range(2)]
        part = jnp.concatenate(part, axis=1)
        for e in range(TILE // FEW):
            out_ref[e * NK + k] = part[e * FEW : (e + 1) * FEW]


def returned_rows(slot_ref, half):
    row = lax.broadcasted_iota(jnp.int32, (TILE, slot_ref.shape[1]), 0)
    return jnp.right_shift(row, 4) * (2 * FEW) + half * FEW + jnp.bitwise_and(row, FEW - 1)


def finish_kernel(slot_ref, back_ref, out_ref):
    feat = out_ref.shape[0]
    slots = []
    for e in range(TILE // FEW):
        total = back_ref[e * NK].astype(F32)
        for k in range(1, NK):
            total = total + back_ref[e * NK + k].astype(F32)
        slots.append(total.astype(BF16))
    slots = jnp.concatenate(slots, axis=0)
    part = [dot(slots, one_hot(slot_ref, returned_rows(slot_ref, h)), TN) for h in range(2)]
    out_ref[...] = (part[0][:feat] + part[1][feat:]).astype(BF16)


def body(tokens, routes, w_gate, w_up, hidden_grad):
    y_at = lax.axis_index("y").astype(jnp.int32).reshape(1)
    zh_at = lax.axis_index("zh").astype(jnp.int32).reshape(1)
    n_groups = lax.axis_size("expert")
    slot_total = hidden_grad.shape[1]
    capacity = slot_total // n_groups
    n_tok, feat = tokens.shape
    block_rows = w_gate.shape[2]
    hid = w_gate.shape[4]
    wide = NZL * feat
    shape = jax.ShapeDtypeStruct

    half = 4 * hid
    gate, up = [
        call(arrange_kernel, shape((block_rows, half), BF16), [], [w[0, 0].reshape(block_rows, half)])
        for w in (w_gate, w_up)
    ]

    packed = call(pack_kernel, shape((NZL, feat // 3, 3 * n_tok), BF16), [], [tokens.T])
    raw = over(("k", "z0"), packed)

    flat_routes = routes.reshape(n_tok * 2)
    named = (flat_routes[:, None] == jnp.arange(n_groups, dtype=jnp.int32)[None, :]).astype(jnp.int32)
    before = jnp.cumsum(named, axis=0) - named
    slot_index = flat_routes * capacity + jnp.sum(before * named, axis=1)
    slot_index = slot_index.reshape(n_tok, 2).T

    raw, gate, up, hidden = lax.optimization_barrier((raw, gate, up, hidden_grad[0]))
    outgoing = call(dispatch_kernel, shape((slot_total, wide), BF16), [], [slot_index, raw])
    arrived = over("expert", outgoing)
    hidden_far = swapped(hidden, "zh")
    rows = gathered("x", arrived)
    rows, hidden_far = lax.optimization_barrier((rows, hidden_far))

    n_flops = 2 * slot_total * block_rows * half
    given = [rows, gate, up]
    send = call(
        functools.partial(forward_kernel, mine=False),
        shape((slot_total, half), BF16),
        [y_at],
        given,
        n_flops,
        16,
    )
    keep = call(
        functools.partial(forward_kernel, mine=True),
        shape((slot_total, half), F32),
        [y_at],
        given,
        n_flops,
        16,
    )
    near = swapped(send, "y")
    send = call(near_kernel, shape((slot_total, half), BF16), [], [keep, near])
    both = gathered("zh", send)

    grads = call(
        grad_kernel,
        shape((slot_total, half), BF16),
        [zh_at],
        [keep, near, both, hidden, hidden_far],
    )
    other = swapped(grads, "y")
    held = call(
        backward_own_kernel,
        shape((NX, slot_total, wide), F32),
        [y_at],
        [grads, gate, up],
        n_flops,
        16,
    )
    pieces = call(
        backward_other_kernel,
        shape((2 * NX, TILE, wide), BF16),
        [y_at],
        [other, gate, up, held],
        n_flops,
        16,
    )
    pieces = over(("z0", "x"), pieces)
    parts = call(sum_kernel, shape((n_groups * NK, FEW, 2 * feat), BF16), [], [pieces])
    parts = over(("expert", "k"), parts)
    total = call(finish_kernel, shape((feat, n_tok), BF16), [], [slot_index, parts])
    return total.T


def solution(mesh):
    tp = AXES[1:]
    cut = Mesh(mesh.devices.reshape(-1, 2, 2, NK, 2, NX), AXES)
    placed = (
        P("expert", tp),
        P("expert", None),
        P("expert", tp, None, None, None),
        P("expert", tp, None, None, None),
        P("expert", None, tp),
    )
    return jax.shard_map(body, mesh=cut, in_specs=placed, out_specs=P("expert", tp), check_vma=False)
```

```python
import functools

import jax
import jax.numpy as jnp
from jax import lax
from jax.experimental import pallas as pl
from jax.experimental.pallas import tpu as pltpu
from jax.sharding import Mesh
from jax.sharding import PartitionSpec as P

NX, NZL, NK = 4, 8, 4
ORDER = [2 * k + z0 for z0 in range(2) for k in range(NK)]
FEW, TILE = 16, 128

AXES = ("expert", "y", "zh", "k", "z0", "x")
F32, BF16 = jnp.float32, jnp.bfloat16
NT = (((1,), (1,)), ((), ()))
TN = (((0,), (0,)), ((), ()))
VMEM = pl.BlockSpec(memory_space=pltpu.VMEM)
SMEM = pl.BlockSpec(memory_space=pltpu.SMEM)


def call(kernel, outs, scalars, arrays, flops=0, mib=6):
    several = isinstance(outs, (tuple, list))
    moved = sum(v.size * v.dtype.itemsize for v in [*arrays, *(outs if several else [outs])])
    return pl.pallas_call(
        kernel,
        out_shape=outs,
        in_specs=[SMEM] * len(scalars) + [VMEM] * len(arrays),
        out_specs=[VMEM] * len(outs) if several else VMEM,
        compiler_params=pltpu.CompilerParams(vmem_limit_bytes=mib * 1024 * 1024),
        cost_estimate=pl.CostEstimate(flops=flops, bytes_accessed=moved, transcendentals=0),
    )(*scalars, *arrays)


def swapped(shard, axis):
    return lax.ppermute(shard, axis, [(0, 1), (1, 0)])


def over(axes, shard):
    return lax.all_to_all(shard, axes, split_axis=0, concat_axis=0, tiled=True)


def gathered(axis, shard):
    return lax.all_gather(shard, axis, axis=0, tiled=False)


def dot(a, b, dims=(((1,), (0,)), ((), ()))):
    return lax.dot_general(a, b, dims, preferred_element_type=F32)


def pack_kernel(tok_ref, out_ref):
    turned = tok_ref[...]
    third = turned.shape[0] // 3
    packed = jnp.concatenate([turned[j * third : (j + 1) * third] for j in range(3)], axis=1)
    for z in range(out_ref.shape[0]):
        out_ref[z] = packed


def arrange_kernel(gate_ref, up_ref, gate_out_ref, up_out_ref):
    feat = gate_ref.shape[0] // (NX * NZL)
    for x in range(NX):
        for at, z in enumerate(ORDER):
            src, dst = (z * NX + x) * feat, (x * NZL + at) * feat
            gate_out_ref[dst : dst + feat] = gate_ref[src : src + feat]
            up_out_ref[dst : dst + feat] = up_ref[src : src + feat]


def slots_of(routes_ref):
    named = routes_ref[...].astype(F32)
    shape = (named.shape[1], named.shape[1])
    before, now = (lax.broadcasted_iota(jnp.int32, shape, axis) for axis in range(2))
    turned = [
        jnp.sum(jnp.where(before == now, named[j : j + 1], 0.0), axis=1, keepdims=True) for j in range(2)
    ]
    slots = []
    for k in range(2):
        own = named[k : k + 1]
        same = jnp.where(turned[0] == own, 1.0, 0.0) + jnp.where(turned[1] == own, 1.0, 0.0)
        place = jnp.sum(jnp.where(before < now, same, 0.0), axis=0, keepdims=True)
        slots.append((own * (2.0 * FEW) + place).astype(jnp.int32))
    return slots


def one_hot(taken, slots):
    return jnp.where((slots == taken[0]) | (slots == taken[1]), 1.0, 0.0).astype(BF16)


def dispatch_kernel(routes_ref, raw_ref, out_ref):
    n_tok = routes_ref.shape[1]
    pieces = [
        raw_ref[z, :, j * n_tok : (j + 1) * n_tok] for z in ORDER for j in range(3)
    ]
    raw = jnp.concatenate(pieces, axis=0)
    slots = lax.broadcasted_iota(jnp.int32, (out_ref.shape[0], n_tok), 0)
    out_ref[...] = dot(one_hot(slots_of(routes_ref), slots), raw, NT).astype(BF16)


def halves(y_ref, width):
    own = pl.multiple_of(y_ref[0] * width, width)
    other = pl.multiple_of((1 - y_ref[0]) * width, width)
    return pl.ds(own, width), pl.ds(other, width)


def forward_kernel(y_ref, rows_ref, gate_ref, up_ref, out_ref, *, mine):
    width = gate_ref.shape[1] // 2
    at = halves(y_ref, width)[0 if mine else 1]
    rows = jnp.concatenate([rows_ref[x] for x in range(rows_ref.shape[0])], axis=1)
    for m, w_ref in enumerate((gate_ref, up_ref)):
        out_ref[:, m * width : (m + 1) * width] = dot(rows, w_ref[:, at]).astype(out_ref.dtype)


def near_kernel(keep_ref, near_ref, send_ref):
    send_ref[...] = (keep_ref[...] + near_ref[...].astype(F32)).astype(BF16)


def grad_kernel(zh_ref, keep_ref, near_ref, both_ref, hid_ref, far_ref, out_ref):
    width = keep_ref.shape[1]
    hid = width // 4
    total = keep_ref[...] + near_ref[...].astype(F32) + both_ref[1 - zh_ref[0]].astype(F32)
    own, far = hid_ref[...].astype(F32), far_ref[...].astype(F32)
    for j in range(2):
        upstream = jnp.where(zh_ref[0] == j, own, far)
        gate_pre = total[:, j * hid : (j + 1) * hid]
        up_pre = total[:, (2 + j) * hid : (3 + j) * hid]
        sig = jax.nn.sigmoid(gate_pre)
        gate_grad = upstream * up_pre * sig * (1.0 + gate_pre * (1.0 - sig))
        out_ref[:, j * hid : (j + 1) * hid] = gate_grad.astype(BF16)
        out_ref[:, (2 + j) * hid : (3 + j) * hid] = (upstream * gate_pre * sig).astype(BF16)


def backward(y_ref, grad_ref, gate_ref, up_ref, x, mine):
    width = gate_ref.shape[1] // 2
    at = halves(y_ref, width)[0 if mine else 1]
    wide = gate_ref.shape[0] // NX
    r = slice(x * wide, (x + 1) * wide)
    return dot(grad_ref[:, :width], gate_ref[r, at], NT) + dot(grad_ref[:, width:], up_ref[r, at], NT)


def backward_own_kernel(y_ref, grad_ref, gate_ref, up_ref, out_ref):
    for x in range(NX):
        out_ref[x] = backward(y_ref, grad_ref, gate_ref, up_ref, x, True)


def backward_other_kernel(y_ref, grad_ref, gate_ref, up_ref, held_ref, out_ref):
    wide = out_ref.shape[2] // 2
    for x in range(NX):
        total = held_ref[x] + backward(y_ref, grad_ref, gate_ref, up_ref, x, False)
        total = total.astype(BF16)
        part = []
        for h in range(2):
            starts = [(2 * e + h) * FEW for e in range(TILE // FEW)]
            part.append(jnp.concatenate([total[v : v + FEW] for v in starts], axis=0))
        for z0 in range(2):
            at = slice(z0 * wide, (z0 + 1) * wide)
            out_ref[z0 * NX + x] = jnp.concatenate([part[0][:, at], part[1][:, at]], axis=1)


def sum_kernel(pieces_ref, out_ref):
    total = pieces_ref[0].astype(F32)
    for m in range(1, pieces_ref.shape[0]):
        total = total + pieces_ref[m].astype(F32)
    total = total.astype(BF16)
    wide = total.shape[1] // 2
    feat = wide // NK
    for k in range(NK):
        part = [total[:, h * wide + k * feat : h * wide + (k + 1) * feat] for h in range(2)]
        part = jnp.concatenate(part, axis=1)
        for e in range(TILE // FEW):
            out_ref[e * NK + k] = part[e * FEW : (e + 1) * FEW]


def returned_rows(n_tok, half):
    row = lax.broadcasted_iota(jnp.int32, (TILE, n_tok), 0)
    return jnp.right_shift(row, 4) * (2 * FEW) + half * FEW + jnp.bitwise_and(row, FEW - 1)


def finish_kernel(routes_ref, back_ref, out_ref):
    feat, n_tok = out_ref.shape
    taken = slots_of(routes_ref)
    slots = []
    for e in range(TILE // FEW):
        total = back_ref[e * NK].astype(F32)
        for k in range(1, NK):
            total = total + back_ref[e * NK + k].astype(F32)
        slots.append(total.astype(BF16))
    slots = jnp.concatenate(slots, axis=0)
    part = [dot(slots, one_hot(taken, returned_rows(n_tok, h)), TN) for h in range(2)]
    out_ref[...] = (part[0][:feat] + part[1][feat:]).astype(BF16)


def body(tokens, routes, w_gate, w_up, hidden_grad):
    y_at = lax.axis_index("y").astype(jnp.int32).reshape(1)
    zh_at = lax.axis_index("zh").astype(jnp.int32).reshape(1)
    n_groups = lax.axis_size("expert")
    slot_total = hidden_grad.shape[1]
    n_tok, feat = tokens.shape
    block_rows = w_gate.shape[2]
    hid = w_gate.shape[4]
    wide = NZL * feat
    shape = jax.ShapeDtypeStruct

    half = 4 * hid
    flat = [w[0, 0].reshape(block_rows, half) for w in (w_gate, w_up)]
    gate, up = call(arrange_kernel, [shape((block_rows, half), BF16)] * 2, [], flat, mib=16)

    packed = call(pack_kernel, shape((NZL, feat // 3, 3 * n_tok), BF16), [], [tokens.T])
    raw = over(("k", "z0"), packed)

    raw, gate, up, hidden = lax.optimization_barrier((raw, gate, up, hidden_grad[0]))
    outgoing = call(dispatch_kernel, shape((slot_total, wide), BF16), [], [routes.T, raw])
    arrived = over("expert", outgoing)
    hidden_far = swapped(hidden, "zh")
    rows = gathered("x", arrived)
    rows, hidden_far = lax.optimization_barrier((rows, hidden_far))

    n_flops = 2 * slot_total * block_rows * half
    given = [rows, gate, up]
    send = call(
        functools.partial(forward_kernel, mine=False),
        shape((slot_total, half), BF16),
        [y_at],
        given,
        n_flops,
        16,
    )
    keep = call(
        functools.partial(forward_kernel, mine=True),
        shape((slot_total, half), F32),
        [y_at],
        given,
        n_flops,
        16,
    )
    near = swapped(send, "y")
    send = call(near_kernel, shape((slot_total, half), BF16), [], [keep, near])
    both = gathered("zh", send)

    grads = call(
        grad_kernel,
        shape((slot_total, half), BF16),
        [zh_at],
        [keep, near, both, hidden, hidden_far],
    )
    other = swapped(grads, "y")
    held = call(
        backward_own_kernel,
        shape((NX, slot_total, wide), F32),
        [y_at],
        [grads, gate, up],
        n_flops,
        16,
    )
    pieces = call(
        backward_other_kernel,
        shape((2 * NX, TILE, wide), BF16),
        [y_at],
        [other, gate, up, held],
        n_flops,
        16,
    )
    pieces = over(("z0", "x"), pieces)
    parts = call(sum_kernel, shape((n_groups * NK, FEW, 2 * feat), BF16), [], [pieces])
    parts = over(("expert", "k"), parts)
    total = call(finish_kernel, shape((feat, n_tok), BF16), [], [routes.T, parts])
    return total.T


def solution(mesh):
    tp = AXES[1:]
    cut = Mesh(mesh.devices.reshape(-1, 2, 2, NK, 2, NX), AXES)
    placed = (
        P("expert", tp),
        P("expert", None),
        P("expert", tp, None, None, None),
        P("expert", tp, None, None, None),
        P("expert", None, tp),
    )
    return jax.shard_map(body, mesh=cut, in_specs=placed, out_specs=P("expert", tp), check_vma=False)
```

```python
import functools

import jax
import jax.numpy as jnp
from jax import lax
from jax.experimental import pallas as pl
from jax.experimental.pallas import tpu as pltpu
from jax.sharding import Mesh
from jax.sharding import PartitionSpec as P

NX, NZL, NK = 4, 8, 4
ORDER = [2 * k + z0 for z0 in range(2) for k in range(NK)]
FEW, TILE = 16, 128

AXES = ("expert", "y", "zh", "k", "z0", "x")
F32, BF16 = jnp.float32, jnp.bfloat16
NT = (((1,), (1,)), ((), ()))
TN = (((0,), (0,)), ((), ()))
VMEM = pl.BlockSpec(memory_space=pltpu.VMEM)
SMEM = pl.BlockSpec(memory_space=pltpu.SMEM)


def call(kernel, outs, scalars, arrays, flops=0, mib=6):
    several = isinstance(outs, (tuple, list))
    moved = sum(v.size * v.dtype.itemsize for v in [*arrays, *(outs if several else [outs])])
    return pl.pallas_call(
        kernel,
        out_shape=outs,
        in_specs=[SMEM] * len(scalars) + [VMEM] * len(arrays),
        out_specs=[VMEM] * len(outs) if several else VMEM,
        compiler_params=pltpu.CompilerParams(vmem_limit_bytes=mib * 1024 * 1024),
        cost_estimate=pl.CostEstimate(flops=flops, bytes_accessed=moved, transcendentals=0),
    )(*scalars, *arrays)


def swapped(shard, axis):
    return lax.ppermute(shard, axis, [(0, 1), (1, 0)])


def over(axes, shard):
    return lax.all_to_all(shard, axes, split_axis=0, concat_axis=0, tiled=True)


def gathered(axis, shard):
    return lax.all_gather(shard, axis, axis=0, tiled=False)


def dot(a, b, dims=(((1,), (0,)), ((), ()))):
    return lax.dot_general(a, b, dims, preferred_element_type=F32)


def arrange_kernel(gate_ref, up_ref, gate_out_ref, up_out_ref):
    feat = gate_ref.shape[0] // (NX * NZL)
    for x in range(NX):
        for at, z in enumerate(ORDER):
            src, dst = (z * NX + x) * feat, (x * NZL + at) * feat
            gate_out_ref[dst : dst + feat] = gate_ref[src : src + feat]
            up_out_ref[dst : dst + feat] = up_ref[src : src + feat]


def slots_of(routes_ref):
    named = routes_ref[...].astype(F32)
    shape = (named.shape[1], named.shape[1])
    before, now = (lax.broadcasted_iota(jnp.int32, shape, axis) for axis in range(2))
    turned = [
        jnp.sum(jnp.where(before == now, named[j : j + 1], 0.0), axis=1, keepdims=True) for j in range(2)
    ]
    slots = []
    for k in range(2):
        own = named[k : k + 1]
        same = jnp.where(turned[0] == own, 1.0, 0.0) + jnp.where(turned[1] == own, 1.0, 0.0)
        place = jnp.sum(jnp.where(before < now, same, 0.0), axis=0, keepdims=True)
        slots.append((own * (2.0 * FEW) + place).astype(jnp.int32))
    return slots


def one_hot(taken, slots):
    return jnp.where((slots == taken[0]) | (slots == taken[1]), 1.0, 0.0).astype(BF16)


def packed_rows(n_tok, half):
    row = lax.broadcasted_iota(jnp.int32, (TILE, n_tok), 0)
    return jnp.right_shift(row, 4) * (2 * FEW) + half * FEW + jnp.bitwise_and(row, FEW - 1)


def dispatch_kernel(routes_ref, tok_ref, out_ref):
    taken = slots_of(routes_ref)
    tokens = tok_ref[...]
    part = [dot(one_hot(taken, packed_rows(tokens.shape[1], h)), tokens, NT) for h in range(2)]
    part = jnp.concatenate(part, axis=1).astype(BF16)
    for e in range(TILE // FEW):
        for k in range(NK):
            out_ref[e * NK + k] = part[e * FEW : (e + 1) * FEW]


def copies_kernel(in_ref, out_ref):
    feat = in_ref.shape[2] // 2
    blocks = [
        jnp.concatenate([in_ref[e * NK + k] for e in range(TILE // FEW)], axis=0) for k in range(NK)
    ]
    lanes = [block[:, h * feat : (h + 1) * feat] for h in range(2) for block in blocks]
    rows = jnp.concatenate(lanes, axis=1)
    for m in range(out_ref.shape[0]):
        out_ref[m] = rows


def halves(y_ref, width):
    own = pl.multiple_of(y_ref[0] * width, width)
    other = pl.multiple_of((1 - y_ref[0]) * width, width)
    return pl.ds(own, width), pl.ds(other, width)


def forward_kernel(y_ref, rows_ref, gate_ref, up_ref, out_ref, *, mine):
    width = gate_ref.shape[1] // 2
    at = halves(y_ref, width)[0 if mine else 1]
    wide = rows_ref.shape[2] // 2
    members = [z0 * NX + x for x in range(NX) for z0 in range(2)]
    rows = [
        jnp.concatenate([rows_ref[m, :, h * wide : (h + 1) * wide] for m in members], axis=1)
        for h in range(2)
    ]
    rows = jnp.concatenate(rows, axis=0)
    for m, w_ref in enumerate((gate_ref, up_ref)):
        out_ref[:, m * width : (m + 1) * width] = dot(rows, w_ref[:, at]).astype(out_ref.dtype)


def near_kernel(keep_ref, near_ref, send_ref):
    send_ref[...] = (keep_ref[...] + near_ref[...].astype(F32)).astype(BF16)


def slot_order(ref):
    starts = [(2 * source + h) * FEW for h in range(2) for source in range(TILE // FEW)]
    return jnp.concatenate([ref[v : v + FEW] for v in starts], axis=0).astype(F32)


def grad_kernel(zh_ref, keep_ref, near_ref, both_ref, hid_ref, far_ref, out_ref):
    width = keep_ref.shape[1]
    hid = width // 4
    total = keep_ref[...] + near_ref[...].astype(F32) + both_ref[1 - zh_ref[0]].astype(F32)
    own, far = slot_order(hid_ref), slot_order(far_ref)
    for j in range(2):
        upstream = jnp.where(zh_ref[0] == j, own, far)
        gate_pre = total[:, j * hid : (j + 1) * hid]
        up_pre = total[:, (2 + j) * hid : (3 + j) * hid]
        sig = jax.nn.sigmoid(gate_pre)
        gate_grad = upstream * up_pre * sig * (1.0 + gate_pre * (1.0 - sig))
        out_ref[:, j * hid : (j + 1) * hid] = gate_grad.astype(BF16)
        out_ref[:, (2 + j) * hid : (3 + j) * hid] = (upstream * gate_pre * sig).astype(BF16)


def backward(y_ref, grad_ref, gate_ref, up_ref, x, mine):
    width = gate_ref.shape[1] // 2
    at = halves(y_ref, width)[0 if mine else 1]
    wide = gate_ref.shape[0] // NX
    r = slice(x * wide, (x + 1) * wide)
    return dot(grad_ref[:, :width], gate_ref[r, at], NT) + dot(grad_ref[:, width:], up_ref[r, at], NT)


def backward_own_kernel(y_ref, grad_ref, gate_ref, up_ref, out_ref):
    for x in range(NX):
        out_ref[x] = backward(y_ref, grad_ref, gate_ref, up_ref, x, True)


def backward_other_kernel(y_ref, grad_ref, gate_ref, up_ref, held_ref, out_ref):
    wide = out_ref.shape[2] // 2
    for x in range(NX):
        total = held_ref[x] + backward(y_ref, grad_ref, gate_ref, up_ref, x, False)
        total = total.astype(BF16)
        part = [total[h * TILE : (h + 1) * TILE] for h in range(2)]
        for z0 in range(2):
            at = slice(z0 * wide, (z0 + 1) * wide)
            out_ref[z0 * NX + x] = jnp.concatenate([part[0][:, at], part[1][:, at]], axis=1)


def sum_kernel(pieces_ref, out_ref):
    total = pieces_ref[0].astype(F32)
    for m in range(1, pieces_ref.shape[0]):
        total = total + pieces_ref[m].astype(F32)
    total = total.astype(BF16)
    wide = total.shape[1] // 2
    feat = wide // NK
    for k in range(NK):
        part = [total[:, h * wide + k * feat : h * wide + (k + 1) * feat] for h in range(2)]
        part = jnp.concatenate(part, axis=1)
        for e in range(TILE // FEW):
            out_ref[e * NK + k] = part[e * FEW : (e + 1) * FEW]


def finish_kernel(routes_ref, back_ref, out_ref):
    feat, n_tok = out_ref.shape
    taken = slots_of(routes_ref)
    slots = []
    for e in range(TILE // FEW):
        total = back_ref[e * NK].astype(F32)
        for k in range(1, NK):
            total = total + back_ref[e * NK + k].astype(F32)
        slots.append(total.astype(BF16))
    slots = jnp.concatenate(slots, axis=0)
    part = [dot(slots, one_hot(taken, packed_rows(n_tok, h)), TN) for h in range(2)]
    out_ref[...] = (part[0][:feat] + part[1][feat:]).astype(BF16)


def body(tokens, routes, w_gate, w_up, hidden_grad):
    y_at = lax.axis_index("y").astype(jnp.int32).reshape(1)
    zh_at = lax.axis_index("zh").astype(jnp.int32).reshape(1)
    n_groups = lax.axis_size("expert")
    slot_total = hidden_grad.shape[1]
    n_tok, feat = tokens.shape
    block_rows = w_gate.shape[2]
    hid = w_gate.shape[4]
    wide = 2 * NK * feat
    shape = jax.ShapeDtypeStruct

    half = 4 * hid
    flat = [w[0, 0].reshape(block_rows, half) for w in (w_gate, w_up)]
    gate, up = call(arrange_kernel, [shape((block_rows, half), BF16)] * 2, [], flat, mib=16)

    sent = call(
        dispatch_kernel, shape((n_groups * NK, FEW, 2 * feat), BF16), [], [routes.T, tokens.T]
    )
    gate, up, hidden = lax.optimization_barrier((gate, up, hidden_grad[0]))
    arrived = over(("expert", "k"), sent)
    hidden_far = swapped(hidden, "zh")
    arrived, gate, up, hidden_far = lax.optimization_barrier((arrived, gate, up, hidden_far))
    copies = call(copies_kernel, shape((2 * NX, TILE, wide), BF16), [], [arrived])
    rows = over(("z0", "x"), copies)

    n_flops = 2 * slot_total * block_rows * half
    given = [rows, gate, up]
    send = call(
        functools.partial(forward_kernel, mine=False),
        shape((slot_total, half), BF16),
        [y_at],
        given,
        n_flops,
        16,
    )
    keep = call(
        functools.partial(forward_kernel, mine=True),
        shape((slot_total, half), F32),
        [y_at],
        given,
        n_flops,
        16,
    )
    near = swapped(send, "y")
    send = call(near_kernel, shape((slot_total, half), BF16), [], [keep, near])
    both = gathered("zh", send)

    grads = call(
        grad_kernel,
        shape((slot_total, half), BF16),
        [zh_at],
        [keep, near, both, hidden, hidden_far],
    )
    other = swapped(grads, "y")
    held = call(
        backward_own_kernel,
        shape((NX, slot_total, wide), F32),
        [y_at],
        [grads, gate, up],
        n_flops,
        16,
    )
    pieces = call(
        backward_other_kernel,
        shape((2 * NX, TILE, wide), BF16),
        [y_at],
        [other, gate, up, held],
        n_flops,
        16,
    )
    pieces = over(("z0", "x"), pieces)
    parts = call(sum_kernel, shape((n_groups * NK, FEW, 2 * feat), BF16), [], [pieces])
    parts = over(("expert", "k"), parts)
    total = call(finish_kernel, shape((feat, n_tok), BF16), [], [routes.T, parts])
    return total.T


def solution(mesh):
    tp = AXES[1:]
    cut = Mesh(mesh.devices.reshape(-1, 2, 2, NK, 2, NX), AXES)
    placed = (
        P("expert", tp),
        P("expert", None),
        P("expert", tp, None, None, None),
        P("expert", tp, None, None, None),
        P("expert", None, tp),
    )
    return jax.shard_map(body, mesh=cut, in_specs=placed, out_specs=P("expert", tp), check_vma=False)
```

```python
import functools

import jax
import jax.numpy as jnp
from jax import lax
from jax.experimental import pallas as pl
from jax.experimental.pallas import tpu as pltpu
from jax.sharding import Mesh
from jax.sharding import PartitionSpec as P

NX, NZL, NK = 4, 8, 4
ORDER = [2 * k + z0 for z0 in range(2) for k in range(NK)]
FEW, TILE = 16, 128

AXES = ("expert", "y", "zh", "k", "z0", "x")
F32, BF16 = jnp.float32, jnp.bfloat16
NT = (((1,), (1,)), ((), ()))
TN = (((0,), (0,)), ((), ()))
VMEM = pl.BlockSpec(memory_space=pltpu.VMEM)
SMEM = pl.BlockSpec(memory_space=pltpu.SMEM)


def call(kernel, outs, scalars, arrays, flops=0, mib=6):
    several = isinstance(outs, (tuple, list))
    moved = sum(v.size * v.dtype.itemsize for v in [*arrays, *(outs if several else [outs])])
    return pl.pallas_call(
        kernel,
        out_shape=outs,
        in_specs=[SMEM] * len(scalars) + [VMEM] * len(arrays),
        out_specs=[VMEM] * len(outs) if several else VMEM,
        compiler_params=pltpu.CompilerParams(vmem_limit_bytes=mib * 1024 * 1024),
        cost_estimate=pl.CostEstimate(flops=flops, bytes_accessed=moved, transcendentals=0),
    )(*scalars, *arrays)


def swapped(shard, axis):
    return lax.ppermute(shard, axis, [(0, 1), (1, 0)])


def over(axes, shard):
    return lax.all_to_all(shard, axes, split_axis=0, concat_axis=0, tiled=True)


def gathered(axis, shard):
    return lax.all_gather(shard, axis, axis=0, tiled=False)


def dot(a, b, dims=(((1,), (0,)), ((), ()))):
    return lax.dot_general(a, b, dims, preferred_element_type=F32)


def pack_kernel(tok_ref, out_ref):
    turned = tok_ref[...]
    third = turned.shape[0] // 3
    packed = jnp.concatenate([turned[j * third : (j + 1) * third] for j in range(3)], axis=1)
    for z in range(out_ref.shape[0]):
        out_ref[z] = packed


def arrange_kernel(gate_ref, up_ref, gate_out_ref, up_out_ref):
    feat = gate_ref.shape[0] // (NX * NZL)
    for x in range(NX):
        for at, z in enumerate(ORDER):
            src, dst = (z * NX + x) * feat, (x * NZL + at) * feat
            gate_out_ref[dst : dst + feat] = gate_ref[src : src + feat]
            up_out_ref[dst : dst + feat] = up_ref[src : src + feat]


def slots_of(routes_ref):
    named = routes_ref[...].astype(F32)
    shape = (named.shape[1], named.shape[1])
    before, now = (lax.broadcasted_iota(jnp.int32, shape, axis) for axis in range(2))
    turned = [
        jnp.sum(jnp.where(before == now, named[j : j + 1], 0.0), axis=1, keepdims=True) for j in range(2)
    ]
    slots = []
    for k in range(2):
        own = named[k : k + 1]
        same = jnp.where(turned[0] == own, 1.0, 0.0) + jnp.where(turned[1] == own, 1.0, 0.0)
        place = jnp.sum(jnp.where(before < now, same, 0.0), axis=0, keepdims=True)
        slots.append((own * (2.0 * FEW) + place).astype(jnp.int32))
    return slots


def one_hot(taken, slots):
    return jnp.where((slots == taken[0]) | (slots == taken[1]), 1.0, 0.0).astype(BF16)


def dispatch_kernel(routes_ref, raw_ref, out_ref):
    n_tok = routes_ref.shape[1]
    pieces = [
        raw_ref[z, :, j * n_tok : (j + 1) * n_tok] for z in ORDER for j in range(3)
    ]
    raw = jnp.concatenate(pieces, axis=0)
    slots = lax.broadcasted_iota(jnp.int32, (out_ref.shape[0], n_tok), 0)
    out_ref[...] = dot(one_hot(slots_of(routes_ref), slots), raw, NT).astype(BF16)


def halves(y_ref, width):
    own = pl.multiple_of(y_ref[0] * width, width)
    other = pl.multiple_of((1 - y_ref[0]) * width, width)
    return pl.ds(own, width), pl.ds(other, width)


def forward_kernel(y_ref, rows_ref, gate_ref, up_ref, out_ref, *, mine):
    width = gate_ref.shape[1] // 2
    at = halves(y_ref, width)[0 if mine else 1]
    rows = jnp.concatenate([rows_ref[x] for x in range(rows_ref.shape[0])], axis=1)
    for m, w_ref in enumerate((gate_ref, up_ref)):
        out_ref[:, m * width : (m + 1) * width] = dot(rows, w_ref[:, at]).astype(out_ref.dtype)


def near_kernel(keep_ref, near_ref, send_ref):
    send_ref[...] = (keep_ref[...] + near_ref[...].astype(F32)).astype(BF16)


def grad_kernel(zh_ref, keep_ref, near_ref, both_ref, hid_ref, far_ref, out_ref):
    width = keep_ref.shape[1]
    hid = width // 4
    total = keep_ref[...] + near_ref[...].astype(F32) + both_ref[1 - zh_ref[0]].astype(F32)
    own, far = hid_ref[...].astype(F32), far_ref[...].astype(F32)
    for j in range(2):
        upstream = jnp.where(zh_ref[0] == j, own, far)
        gate_pre = total[:, j * hid : (j + 1) * hid]
        up_pre = total[:, (2 + j) * hid : (3 + j) * hid]
        sig = jax.nn.sigmoid(gate_pre)
        gate_grad = upstream * up_pre * sig * (1.0 + gate_pre * (1.0 - sig))
        out_ref[:, j * hid : (j + 1) * hid] = gate_grad.astype(BF16)
        out_ref[:, (2 + j) * hid : (3 + j) * hid] = (upstream * gate_pre * sig).astype(BF16)


def backward(y_ref, grad_ref, gate_ref, up_ref, x, mine):
    width = gate_ref.shape[1] // 2
    at = halves(y_ref, width)[0 if mine else 1]
    wide = gate_ref.shape[0] // NX
    r = slice(x * wide, (x + 1) * wide)
    return dot(grad_ref[:, :width], gate_ref[r, at], NT) + dot(grad_ref[:, width:], up_ref[r, at], NT)


def backward_own_kernel(y_ref, grad_ref, gate_ref, up_ref, out_ref):
    for x in range(NX):
        out_ref[x] = backward(y_ref, grad_ref, gate_ref, up_ref, x, True)


def backward_other_kernel(y_ref, grad_ref, gate_ref, up_ref, held_ref, out_ref):
    wide = out_ref.shape[2] // 2
    for x in range(NX):
        total = held_ref[x] + backward(y_ref, grad_ref, gate_ref, up_ref, x, False)
        total = total.astype(BF16)
        part = []
        for h in range(2):
            starts = [(2 * e + h) * FEW for e in range(TILE // FEW)]
            part.append(jnp.concatenate([total[v : v + FEW] for v in starts], axis=0))
        for z0 in range(2):
            at = slice(z0 * wide, (z0 + 1) * wide)
            out_ref[z0 * NX + x] = jnp.concatenate([part[0][:, at], part[1][:, at]], axis=1)


def sum_kernel(pieces_ref, out_ref):
    total = pieces_ref[0].astype(F32)
    for m in range(1, pieces_ref.shape[0]):
        total = total + pieces_ref[m].astype(F32)
    total = total.astype(BF16)
    wide = total.shape[1] // 2
    feat = wide // NK
    for k in range(NK):
        part = [total[:, h * wide + k * feat : h * wide + (k + 1) * feat] for h in range(2)]
        part = jnp.concatenate(part, axis=1)
        for e in range(TILE // FEW):
            out_ref[e * NK + k] = part[e * FEW : (e + 1) * FEW]


def returned_rows(n_tok, half):
    row = lax.broadcasted_iota(jnp.int32, (TILE, n_tok), 0)
    return jnp.right_shift(row, 4) * (2 * FEW) + half * FEW + jnp.bitwise_and(row, FEW - 1)


def finish_kernel(routes_ref, back_ref, out_ref):
    feat, n_tok = out_ref.shape
    taken = slots_of(routes_ref)
    slots = []
    for e in range(TILE // FEW):
        total = back_ref[e * NK].astype(F32)
        for k in range(1, NK):
            total = total + back_ref[e * NK + k].astype(F32)
        slots.append(total)
    slots = jnp.concatenate(slots, axis=0)
    high = slots.astype(BF16)
    low = (slots - high.astype(F32)).astype(BF16)
    part = []
    for h in range(2):
        placing = one_hot(taken, returned_rows(n_tok, h))
        part.append(dot(high, placing, TN) + dot(low, placing, TN))
    out_ref[...] = (part[0][:feat] + part[1][feat:]).astype(BF16)


def body(tokens, routes, w_gate, w_up, hidden_grad):
    y_at = lax.axis_index("y").astype(jnp.int32).reshape(1)
    zh_at = lax.axis_index("zh").astype(jnp.int32).reshape(1)
    n_groups = lax.axis_size("expert")
    slot_total = hidden_grad.shape[1]
    n_tok, feat = tokens.shape
    block_rows = w_gate.shape[2]
    hid = w_gate.shape[4]
    wide = NZL * feat
    shape = jax.ShapeDtypeStruct

    half = 4 * hid
    flat = [w[0, 0].reshape(block_rows, half) for w in (w_gate, w_up)]
    gate, up = call(arrange_kernel, [shape((block_rows, half), BF16)] * 2, [], flat, mib=16)

    packed = call(pack_kernel, shape((NZL, feat // 3, 3 * n_tok), BF16), [], [tokens.T])
    raw = over(("k", "z0"), packed)

    raw, gate, up, hidden = lax.optimization_barrier((raw, gate, up, hidden_grad[0]))
    outgoing = call(dispatch_kernel, shape((slot_total, wide), BF16), [], [routes.T, raw])
    arrived = over("expert", outgoing)
    hidden_far = swapped(hidden, "zh")
    rows = gathered("x", arrived)
    rows, hidden_far = lax.optimization_barrier((rows, hidden_far))

    n_flops = 2 * slot_total * block_rows * half
    given = [rows, gate, up]
    send = call(
        functools.partial(forward_kernel, mine=False),
        shape((slot_total, half), BF16),
        [y_at],
        given,
        n_flops,
        16,
    )
    keep = call(
        functools.partial(forward_kernel, mine=True),
        shape((slot_total, half), F32),
        [y_at],
        given,
        n_flops,
        16,
    )
    near = swapped(send, "y")
    send = call(near_kernel, shape((slot_total, half), BF16), [], [keep, near])
    both = gathered("zh", send)

    grads = call(
        grad_kernel,
        shape((slot_total, half), BF16),
        [zh_at],
        [keep, near, both, hidden, hidden_far],
    )
    other = swapped(grads, "y")
    held = call(
        backward_own_kernel,
        shape((NX, slot_total, wide), F32),
        [y_at],
        [grads, gate, up],
        n_flops,
        16,
    )
    pieces = call(
        backward_other_kernel,
        shape((2 * NX, TILE, wide), BF16),
        [y_at],
        [other, gate, up, held],
        n_flops,
        16,
    )
    pieces = over(("z0", "x"), pieces)
    parts = call(sum_kernel, shape((n_groups * NK, FEW, 2 * feat), BF16), [], [pieces])
    parts = over(("expert", "k"), parts)
    total = call(finish_kernel, shape((feat, n_tok), BF16), [], [routes.T, parts])
    return total.T


def solution(mesh):
    tp = AXES[1:]
    cut = Mesh(mesh.devices.reshape(-1, 2, 2, NK, 2, NX), AXES)
    placed = (
        P("expert", tp),
        P("expert", None),
        P("expert", tp, None, None, None),
        P("expert", tp, None, None, None),
        P("expert", None, tp),
    )
    return jax.shard_map(body, mesh=cut, in_specs=placed, out_specs=P("expert", tp), check_vma=False)
```

```python
import functools

import jax
import jax.numpy as jnp
from jax import lax
from jax.experimental import pallas as pl
from jax.experimental.pallas import tpu as pltpu
from jax.sharding import Mesh
from jax.sharding import PartitionSpec as P

NX, NZL, NK = 4, 8, 4
ORDER = [2 * k + z0 for z0 in range(2) for k in range(NK)]
FEW, TILE = 16, 128

AXES = ("expert", "y", "zh", "k", "z0", "x")
F32, BF16 = jnp.float32, jnp.bfloat16
NT = (((1,), (1,)), ((), ()))
TN = (((0,), (0,)), ((), ()))
VMEM = pl.BlockSpec(memory_space=pltpu.VMEM)
SMEM = pl.BlockSpec(memory_space=pltpu.SMEM)


def call(kernel, outs, scalars, arrays, flops=0, mib=6):
    several = isinstance(outs, (tuple, list))
    moved = sum(v.size * v.dtype.itemsize for v in [*arrays, *(outs if several else [outs])])
    return pl.pallas_call(
        kernel,
        out_shape=outs,
        in_specs=[SMEM] * len(scalars) + [VMEM] * len(arrays),
        out_specs=[VMEM] * len(outs) if several else VMEM,
        compiler_params=pltpu.CompilerParams(vmem_limit_bytes=mib * 1024 * 1024),
        cost_estimate=pl.CostEstimate(flops=flops, bytes_accessed=moved, transcendentals=0),
    )(*scalars, *arrays)


def swapped(shard, axis):
    return lax.ppermute(shard, axis, [(0, 1), (1, 0)])


def over(axes, shard):
    return lax.all_to_all(shard, axes, split_axis=0, concat_axis=0, tiled=True)


def gathered(axis, shard):
    return lax.all_gather(shard, axis, axis=0, tiled=False)


def dot(a, b, dims=(((1,), (0,)), ((), ()))):
    return lax.dot_general(a, b, dims, preferred_element_type=F32)


def pack_kernel(tok_ref, out_ref, held_ref, done):
    fetch = pltpu.make_async_copy(tok_ref, held_ref, done)
    fetch.start()
    fetch.wait()
    turned = held_ref[...]
    third = turned.shape[0] // 3
    packed = jnp.concatenate([turned[j * third : (j + 1) * third] for j in range(3)], axis=1)
    for z in range(out_ref.shape[0]):
        out_ref[z] = packed


def arrange_kernel(gate_ref, up_ref, gate_out_ref, up_out_ref):
    feat = gate_ref.shape[0] // (NX * NZL)
    for x in range(NX):
        for at, z in enumerate(ORDER):
            src, dst = (z * NX + x) * feat, (x * NZL + at) * feat
            gate_out_ref[dst : dst + feat] = gate_ref[src : src + feat]
            up_out_ref[dst : dst + feat] = up_ref[src : src + feat]


def slots_of(routes_ref):
    named = routes_ref[...].astype(F32)
    shape = (named.shape[1], named.shape[1])
    before, now = (lax.broadcasted_iota(jnp.int32, shape, axis) for axis in range(2))
    turned = [
        jnp.sum(jnp.where(before == now, named[j : j + 1], 0.0), axis=1, keepdims=True) for j in range(2)
    ]
    slots = []
    for k in range(2):
        own = named[k : k + 1]
        same = jnp.where(turned[0] == own, 1.0, 0.0) + jnp.where(turned[1] == own, 1.0, 0.0)
        place = jnp.sum(jnp.where(before < now, same, 0.0), axis=0, keepdims=True)
        slots.append((own * (2.0 * FEW) + place).astype(jnp.int32))
    return slots


def one_hot(taken, slots):
    return jnp.where((slots == taken[0]) | (slots == taken[1]), 1.0, 0.0).astype(BF16)


def dispatch_kernel(routes_ref, raw_ref, out_ref):
    n_tok = routes_ref.shape[1]
    pieces = [
        raw_ref[z, :, j * n_tok : (j + 1) * n_tok] for z in ORDER for j in range(3)
    ]
    raw = jnp.concatenate(pieces, axis=0)
    slots = lax.broadcasted_iota(jnp.int32, (out_ref.shape[0], n_tok), 0)
    out_ref[...] = dot(one_hot(slots_of(routes_ref), slots), raw, NT).astype(BF16)


def halves(y_ref, width):
    own = pl.multiple_of(y_ref[0] * width, width)
    other = pl.multiple_of((1 - y_ref[0]) * width, width)
    return pl.ds(own, width), pl.ds(other, width)


def forward_kernel(y_ref, rows_ref, gate_ref, up_ref, out_ref, *, mine):
    width = gate_ref.shape[1] // 2
    at = halves(y_ref, width)[0 if mine else 1]
    rows = jnp.concatenate([rows_ref[x] for x in range(rows_ref.shape[0])], axis=1)
    for m, w_ref in enumerate((gate_ref, up_ref)):
        out_ref[:, m * width : (m + 1) * width] = dot(rows, w_ref[:, at]).astype(out_ref.dtype)


def near_kernel(keep_ref, near_ref, send_ref):
    send_ref[...] = (keep_ref[...] + near_ref[...].astype(F32)).astype(BF16)


def grad_kernel(zh_ref, keep_ref, near_ref, both_ref, hid_ref, far_ref, out_ref):
    width = keep_ref.shape[1]
    hid = width // 4
    total = keep_ref[...] + near_ref[...].astype(F32) + both_ref[1 - zh_ref[0]].astype(F32)
    own, far = hid_ref[...].astype(F32), far_ref[...].astype(F32)
    for j in range(2):
        upstream = jnp.where(zh_ref[0] == j, own, far)
        gate_pre = total[:, j * hid : (j + 1) * hid]
        up_pre = total[:, (2 + j) * hid : (3 + j) * hid]
        sig = jax.nn.sigmoid(gate_pre)
        gate_grad = upstream * up_pre * sig * (1.0 + gate_pre * (1.0 - sig))
        out_ref[:, j * hid : (j + 1) * hid] = gate_grad.astype(BF16)
        out_ref[:, (2 + j) * hid : (3 + j) * hid] = (upstream * gate_pre * sig).astype(BF16)


def backward(y_ref, grad_ref, gate_ref, up_ref, x, mine):
    width = gate_ref.shape[1] // 2
    at = halves(y_ref, width)[0 if mine else 1]
    wide = gate_ref.shape[0] // NX
    r = slice(x * wide, (x + 1) * wide)
    return dot(grad_ref[:, :width], gate_ref[r, at], NT) + dot(grad_ref[:, width:], up_ref[r, at], NT)


def backward_own_kernel(y_ref, grad_ref, gate_ref, up_ref, out_ref):
    for x in range(NX):
        out_ref[x] = backward(y_ref, grad_ref, gate_ref, up_ref, x, True)


def backward_other_kernel(y_ref, grad_ref, gate_ref, up_ref, held_ref, out_ref):
    wide = out_ref.shape[2] // 2
    for x in range(NX):
        total = held_ref[x] + backward(y_ref, grad_ref, gate_ref, up_ref, x, False)
        total = total.astype(BF16)
        part = []
        for h in range(2):
            starts = [(2 * e + h) * FEW for e in range(TILE // FEW)]
            part.append(jnp.concatenate([total[v : v + FEW] for v in starts], axis=0))
        for z0 in range(2):
            at = slice(z0 * wide, (z0 + 1) * wide)
            out_ref[z0 * NX + x] = jnp.concatenate([part[0][:, at], part[1][:, at]], axis=1)


def sum_kernel(pieces_ref, out_ref):
    total = pieces_ref[0].astype(F32)
    for m in range(1, pieces_ref.shape[0]):
        total = total + pieces_ref[m].astype(F32)
    total = total.astype(BF16)
    wide = total.shape[1] // 2
    feat = wide // NK
    for k in range(NK):
        part = [total[:, h * wide + k * feat : h * wide + (k + 1) * feat] for h in range(2)]
        part = jnp.concatenate(part, axis=1)
        for e in range(TILE // FEW):
            out_ref[e * NK + k] = part[e * FEW : (e + 1) * FEW]


def returned_rows(n_tok, half):
    row = lax.broadcasted_iota(jnp.int32, (TILE, n_tok), 0)
    return jnp.right_shift(row, 4) * (2 * FEW) + half * FEW + jnp.bitwise_and(row, FEW - 1)


def finish_kernel(routes_ref, back_ref, out_ref):
    feat, n_tok = out_ref.shape
    taken = slots_of(routes_ref)
    slots = []
    for e in range(TILE // FEW):
        total = back_ref[e * NK].astype(F32)
        for k in range(1, NK):
            total = total + back_ref[e * NK + k].astype(F32)
        slots.append(total)
    slots = jnp.concatenate(slots, axis=0)
    high = slots.astype(BF16)
    low = (slots - high.astype(F32)).astype(BF16)
    part = []
    for h in range(2):
        placing = one_hot(taken, returned_rows(n_tok, h))
        part.append(dot(high, placing, TN) + dot(low, placing, TN))
    out_ref[...] = (part[0][:feat] + part[1][feat:]).astype(BF16)


def body(tokens, routes, w_gate, w_up, hidden_grad):
    y_at = lax.axis_index("y").astype(jnp.int32).reshape(1)
    zh_at = lax.axis_index("zh").astype(jnp.int32).reshape(1)
    n_groups = lax.axis_size("expert")
    slot_total = hidden_grad.shape[1]
    n_tok, feat = tokens.shape
    block_rows = w_gate.shape[2]
    hid = w_gate.shape[4]
    wide = NZL * feat
    shape = jax.ShapeDtypeStruct

    half = 4 * hid
    flat = [w[0, 0].reshape(block_rows, half) for w in (w_gate, w_up)]
    gate, up = call(arrange_kernel, [shape((block_rows, half), BF16)] * 2, [], flat, mib=16)

    packed = pl.pallas_call(
        pack_kernel,
        out_shape=shape((NZL, feat // 3, 3 * n_tok), BF16),
        in_specs=[pl.BlockSpec(memory_space=pl.ANY)],
        out_specs=VMEM,
        scratch_shapes=[pltpu.VMEM((feat, n_tok), BF16), pltpu.SemaphoreType.DMA],
        compiler_params=pltpu.CompilerParams(vmem_limit_bytes=56 * 1024 * 1024),
    )(tokens.T)
    raw = over(("k", "z0"), packed)

    raw, gate, up, hidden = lax.optimization_barrier((raw, gate, up, hidden_grad[0]))
    outgoing = call(dispatch_kernel, shape((slot_total, wide), BF16), [], [routes.T, raw])
    arrived = over("expert", outgoing)
    hidden_far = swapped(hidden, "zh")
    rows = gathered("x", arrived)
    rows, hidden_far = lax.optimization_barrier((rows, hidden_far))

    n_flops = 2 * slot_total * block_rows * half
    given = [rows, gate, up]
    send = call(
        functools.partial(forward_kernel, mine=False),
        shape((slot_total, half), BF16),
        [y_at],
        given,
        n_flops,
        16,
    )
    keep = call(
        functools.partial(forward_kernel, mine=True),
        shape((slot_total, half), F32),
        [y_at],
        given,
        n_flops,
        16,
    )
    near = swapped(send, "y")
    send = call(near_kernel, shape((slot_total, half), BF16), [], [keep, near])
    both = gathered("zh", send)

    grads = call(
        grad_kernel,
        shape((slot_total, half), BF16),
        [zh_at],
        [keep, near, both, hidden, hidden_far],
    )
    other = swapped(grads, "y")
    held = call(
        backward_own_kernel,
        shape((NX, slot_total, wide), F32),
        [y_at],
        [grads, gate, up],
        n_flops,
        16,
    )
    pieces = call(
        backward_other_kernel,
        shape((2 * NX, TILE, wide), BF16),
        [y_at],
        [other, gate, up, held],
        n_flops,
        16,
    )
    pieces = over(("z0", "x"), pieces)
    parts = call(sum_kernel, shape((n_groups * NK, FEW, 2 * feat), BF16), [], [pieces])
    parts = over(("expert", "k"), parts)
    total = call(finish_kernel, shape((feat, n_tok), BF16), [], [routes.T, parts])
    return total.T


def solution(mesh):
    tp = AXES[1:]
    cut = Mesh(mesh.devices.reshape(-1, 2, 2, NK, 2, NX), AXES)
    placed = (
        P("expert", tp),
        P("expert", None),
        P("expert", tp, None, None, None),
        P("expert", tp, None, None, None),
        P("expert", None, tp),
    )
    return jax.shard_map(body, mesh=cut, in_specs=placed, out_specs=P("expert", tp), check_vma=False)
```
